512 devices in a mesh: leaf: 128 (over z, x, core), sub: 4 (over y).
Axes of the slice: x: 4, y: 4, z: 16, core: 2. Of those that a mesh axis runs over, the one named last changes fastest.
Arguments:
- points: float32 [3, 2097152], P(None, ('leaf', 'sub')), may hold values from -6 to 6
- charges: bfloat16 [8, 2097152], P(None, ('leaf', 'sub')), may hold values from -6 to 6
- order: int32 [2097152], P(('leaf', 'sub')), may hold values from 0 to 4095, as said below
- basis: bfloat16 [8192, 64, 256], P(('leaf', 'sub')), may hold values from -0.5 to 0.5
- transfer: float32 [8192, 64, 64], P(('leaf', 'sub')), may hold values from -0.375 to 0.375
- leaf_proxy: float32 [8192, 3, 64], P(('leaf', 'sub')), may hold values from -6 to 6
- cluster_proxy: float32 [512, 3, 64], P(('leaf', 'sub')), may hold values from -6 to 6
- near: int32 [8192, 5], P(('leaf', 'sub')), may hold values from -1 to 8191, as said below
- far_leaf: int32 [8192, 8], P(('leaf', 'sub')), may hold values from -1 to 8191, as said below
- far_cluster: int32 [512, 16], P(('leaf', 'sub')), may hold values from -1 to 511, as said below
Outputs:
- potential: float32 [8, 2097152], P(None, ('leaf', 'sub'))
The draws below stay inside these ranges and needn't reach their ends.
Inputs may be any that keep to these rules, and one draw needn't show every extreme that they name: `order`: in each aligned block of 4096 tree positions the entries are a permutation of 0 to 4095. `near`: row g lists distinct leaves h with |h - g| <= 2, g among them, valid entries first and then -1; some row has no -1. `far_leaf`: row g lists distinct leaves h with 2 < |h - g| <= 6, valid entries first and then -1; some row has no -1. `far_cluster`: row c lists distinct clusters of other groups at most 4 groups away from c's group, a group being the 4 clusters c // 4 * 4 to c // 4 * 4 + 3; valid entries first and then -1; some row has no -1.
All inputs are finite; a program needn't handle non-finite values.
Results may differ from the reference program's by a relative error of at most 0.0019.
Values sent between devices are 32-bit elements; how exact they have to be, the bound alone decides.
No kernel may reach another device: no remote copies, remote signals or barrier semaphores. Data moves between devices by JAX's collectives and lax.ppermute only.
A program may use at most 64 MiB of HBM per device.

```python
import jax
import jax.numpy as jnp
from jax import lax

LEAF = 256
RANK = 64
NRHS = 8
REACH = 2
BAND = 4
FAR1 = 16
LEAF_DEV = 16
NEAR = 5
FREACH = 6
FAR0 = 8
PTS_DEV = 4096
NSUB = 4
NGROUP = 128
NCLUS = 512
NLEAF = 8192
NPTS = 2097152


def compact_rows(valid, candidate, scores):
    keys = (1 - valid) * 2 ** 27 + scores
    ranked = jnp.argsort(keys, axis=1, stable=True)
    marked = jnp.where(valid == 1, candidate, -1)
    return jnp.take_along_axis(marked, ranked, axis=1).astype(jnp.int32)


def leaf_lists(key, offsets):
    key_level, key_coin = jax.random.split(key)
    leaves = jnp.arange(NLEAF, dtype=jnp.int32)[:, None]
    candidate = leaves + offsets[None, :]
    level = jax.random.randint(key_level, (NLEAF // LEAF_DEV,), 1, 5)
    density = jnp.repeat(level, LEAF_DEV)[:, None]
    coin = jax.random.randint(key_coin, (NLEAF, offsets.shape[0]), 0, 4)
    chosen = (coin < density) | (offsets[None, :] == 0) | (leaves == NLEAF // 2)
    valid = (chosen & (candidate >= 0) & (candidate < NLEAF)).astype(jnp.int32)
    scores = jnp.zeros_like(valid)
    return compact_rows(valid, candidate, scores)


def draw_near(key, part):
    key = jax.random.fold_in(key, 11)
    offsets = jnp.arange(-REACH, REACH + 1, dtype=jnp.int32)
    return leaf_lists(key, offsets)


def draw_far_leaf(key, part):
    key = jax.random.fold_in(key, 23)
    offsets = jnp.concatenate([jnp.arange(-FREACH, -REACH, dtype=jnp.int32), jnp.arange(REACH + 1, FREACH + 1, dtype=jnp.int32)])
    return leaf_lists(key, offsets)


def draw_far_cluster(key, part):
    key = jax.random.fold_in(key, 37)
    key_coin, key_score = jax.random.split(key)
    steps = jnp.concatenate([jnp.arange(-BAND, 0, dtype=jnp.int32), jnp.arange(1, BAND + 1, dtype=jnp.int32)])
    group_step = jnp.repeat(steps, NSUB)
    member = jnp.tile(jnp.arange(NSUB, dtype=jnp.int32), 2 * BAND)
    clusters = jnp.arange(NCLUS, dtype=jnp.int32)[:, None]
    target_group = clusters // NSUB + group_step[None, :]
    candidate = target_group * NSUB + member[None, :]
    width = 2 * BAND * NSUB
    coin = jax.random.randint(key_coin, (NCLUS, width), 0, 4)
    chosen = (coin < 2) | (clusters == NCLUS // 2)
    valid = (chosen & (target_group >= 0) & (target_group < NGROUP)).astype(jnp.int32)
    scores = jax.random.randint(key_score, (NCLUS, width), 0, 2 ** 20) * 64 + jnp.arange(width, dtype=jnp.int32)[None, :]
    picked = compact_rows(valid, candidate, scores)
    return picked[:, :FAR1]


def draw_order(key, part):
    key = jax.random.fold_in(key, 53)
    keys = jax.random.split(key, NCLUS)
    blocks = jax.vmap(lambda k: jax.random.permutation(k, PTS_DEV))(keys).astype(jnp.int32)
    return blocks.reshape(NPTS)


def block_levels(own_key, shape, cuts, low, top_value):
    factor_of = 1.0
    for axis_at, blocks in cuts:
        steps = jax.random.uniform(jax.random.fold_in(jax.random.fold_in(own_key, 6), axis_at), (blocks,), jnp.float32, low / len(cuts), top_value / len(cuts))
        factor_of = factor_of * jnp.repeat(jnp.exp(steps), shape[axis_at] // blocks).reshape((-1,) + (1,) * (len(shape) - 1 - axis_at))
    return factor_of


def normal_values(rng, shape, scale, bound, cuts=(), held_as=jnp.bfloat16):
    array = jax.random.normal(rng, shape, jnp.float32) * scale
    if len(cuts) > 0:
        array = block_levels(rng, shape, cuts, -0.22, 0.18) * array
    return jnp.clip(array, min=-bound, max=bound).astype(held_as)


def setup_inputs(seed: int = 0) -> dict:
    arg_keys = jax.random.split(jax.random.key(seed), 11)
    return {
        "points": normal_values(arg_keys[0], (3, NPTS), 1.0, 6.0, ((1, 512),), jnp.float32),
        "charges": normal_values(arg_keys[1], (NRHS, NPTS), 1.0, 6.0, ((1, 512),)),
        "order": draw_order(jax.random.fold_in(arg_keys[10], 71), 0),
        "basis": normal_values(arg_keys[3], (NLEAF, RANK, LEAF), (2 * RANK) ** -0.5, 0.5, ((0, 512),)),
        "transfer": normal_values(arg_keys[4], (NLEAF, RANK, RANK), (4 * RANK) ** -0.5, 0.375, ((0, 512),), jnp.float32),
        "leaf_proxy": normal_values(arg_keys[5], (NLEAF, 3, RANK), 1.0, 6.0, ((0, 512),), jnp.float32),
        "cluster_proxy": normal_values(arg_keys[6], (NCLUS, 3, RANK), 1.0, 6.0, ((0, 512),), jnp.float32),
        "near": draw_near(jax.random.fold_in(arg_keys[10], 71), 0),
        "far_leaf": draw_far_leaf(jax.random.fold_in(arg_keys[10], 71), 0),
        "far_cluster": draw_far_cluster(jax.random.fold_in(arg_keys[10], 71), 0),
    }


KERNEL_FACTOR = 0.0625
SMOOTHING_SQUARE = 0.01

def kern(source, target):
    difference_x = source[..., 0, :, None] - target[..., 0, None, :]
    difference_y = source[..., 1, :, None] - target[..., 1, None, :]
    difference_z = source[..., 2, :, None] - target[..., 2, None, :]
    return KERNEL_FACTOR / jnp.sqrt(difference_x * difference_x + difference_y * difference_y + difference_z * difference_z + SMOOTHING_SQUARE)

def reference(points, charges, order, basis, transfer, leaf_proxy, cluster_proxy, near, far_leaf, far_cluster):
    highest_level = lax.Precision.HIGHEST
    block_start = jnp.arange(NPTS, dtype=jnp.int32) // PTS_DEV * PTS_DEV
    source = (order.astype(jnp.int32) + block_start).astype(jnp.int32)
    tree_charges = jnp.take(charges, source, axis=1)
    tree_points = jnp.take(points, source, axis=1)
    leaf_charges = tree_charges.reshape(NRHS, NLEAF, LEAF).transpose(1, 0, 2)
    leaf_points = tree_points.reshape(3, NLEAF, LEAF).transpose(1, 0, 2)
    coeffs = jnp.einsum('glp,grp->glr', leaf_charges.astype(jnp.float32), basis.astype(jnp.float32), precision=highest_level)
    parent_index = jnp.einsum('cglr,cgrs->cls', coeffs.reshape(NCLUS, LEAF_DEV, NRHS, RANK), transfer.reshape(NCLUS, LEAF_DEV, RANK, RANK), precision=highest_level)
    coupled_blocks = jnp.zeros((NCLUS, NRHS, RANK), jnp.float32)
    for slot in range(FAR1):
        target = far_cluster[:, slot]
        valid = target >= 0
        safe_distance = jnp.where(valid, target, 0).astype(jnp.int32)
        keep_mask = valid.astype(jnp.float32)[:, None, None]
        coupling_matrix = kern(jnp.take(cluster_proxy, safe_distance, axis=0), cluster_proxy)
        coupled_blocks = coupled_blocks + jnp.einsum('jub,jbn->jun', jnp.take(parent_index, safe_distance, axis=0) * keep_mask, coupling_matrix, precision=highest_level)
    down = jnp.zeros((NLEAF, NRHS, RANK), jnp.float32)
    for slot in range(FAR0):
        target = far_leaf[:, slot]
        valid = target >= 0
        safe_distance = jnp.where(valid, target, 0).astype(jnp.int32)
        keep_mask = valid.astype(jnp.float32)[:, None, None]
        coupling_matrix = kern(jnp.take(leaf_proxy, safe_distance, axis=0), leaf_proxy)
        down = down + jnp.einsum('glr,grs->gls', jnp.take(coeffs, safe_distance, axis=0) * keep_mask, coupling_matrix, precision=highest_level)
    spread = jnp.repeat(coupled_blocks, LEAF_DEV, axis=0)
    down = down + jnp.einsum('gls,grs->glr', spread, transfer, precision=highest_level)
    far_field = jnp.einsum('glr,grp->glp', down, basis.astype(jnp.float32), precision=highest_level)

    def near_group(args):
        rows, owned = args
        own_points = jnp.take(leaf_points, owned, axis=0)
        total = jnp.zeros((LEAF_DEV, NRHS, LEAF), jnp.float32)
        for slot in range(NEAR):
            target = rows[:, slot]
            valid = target >= 0
            safe_distance = jnp.where(valid, target, 0).astype(jnp.int32)
            dense = kern(jnp.take(leaf_points, safe_distance, axis=0), own_points).astype(jnp.bfloat16)
            weights = jnp.take(leaf_charges, safe_distance, axis=0) * valid.astype(jnp.bfloat16)[:, None, None]
            total = total + jnp.einsum('glp,gpq->glq', weights.astype(jnp.float32), dense.astype(jnp.float32), precision=highest_level)
        return total
    owned_ids = jnp.arange(NLEAF, dtype=jnp.int32).reshape(NCLUS, LEAF_DEV)
    near_sum = lax.map(near_group, (near.reshape(NCLUS, LEAF_DEV, NEAR), owned_ids)).reshape(NLEAF, NRHS, LEAF)
    result = near_sum + far_field
    return result.transpose(1, 0, 2).reshape(NRHS, NPTS)
```

```python
import jax
import jax.numpy as jnp
from jax import lax
from jax.experimental import pallas as pl
from jax.experimental.pallas import tpu as pltpu
from jax.sharding import PartitionSpec as P

LEAF = 256
RANK = 64
NRHS = 8
OWN = 16
REACH = 2
FREACH = 6
PLANE = 8
HALF = PLANE // 2
NSUB = 4
PTS = OWN * LEAF
RANKS = OWN * RANK
LANES = 128
SCALE = 16.0
SHIFT = 2.56

NEAR_W = REACH * LEAF
FAR_W = FREACH * RANK
MSG = 2 * NEAR_W + 2 * FAR_W
AT_CHARGES, AT_POINTS, AT_COEFFS, AT_PROXY = 0, PTS, 2 * PTS, 2 * PTS + RANKS
OWN_W = 2 * PTS + 2 * RANKS

NT = (((1,), (1,)), ((), ()))
NN = (((1,), (0,)), ((), ()))


def dot(a, b, dims=NN):
    return lax.dot_general(a, b, dims, preferred_element_type=jnp.float32)


def split(x):
    high = x.astype(jnp.bfloat16)
    return high, (x - high.astype(jnp.float32)).astype(jnp.bfloat16)


def dot3(a, b, dims=NN):
    rows = a.shape[0]
    a_high, a_low = split(a)
    b_high, b_low = split(b)
    both = dot(jnp.concatenate([a_high, a_low], axis=0), b_high, dims)
    return both[:rows] + both[rows:] + dot(a_high, b_low, dims)


def prepare_kernel(
    charges, points, order, basis, transfer, leaf_proxy, cluster_proxy,
    own, right, left, entry, source,
):
    source[0:NRHS, :] = charges[...].astype(jnp.float32)
    source[NRHS : 2 * NRHS, :] = jnp.zeros((NRHS, PTS), jnp.float32)
    source[NRHS : NRHS + 3, :] = points[...] * SCALE

    def gather(block, carry):
        index = jnp.broadcast_to(order[pl.ds(block, 1), :], (8, LANES))
        high = lax.shift_right_logical(index, 7)
        low = jnp.bitwise_and(index, LANES - 1)
        lanes = pl.ds(pl.multiple_of(block * LANES, LANES), LANES)
        got = [None, None]
        for k in range(PTS // LANES):
            here = high == k
            for part in range(2):
                piece = source[8 * part : 8 * part + 8, k * LANES : (k + 1) * LANES]
                piece = jnp.take_along_axis(piece, low, axis=1)
                got[part] = piece if k == 0 else jnp.where(here, piece, got[part])
        own[:, lanes] = got[0]
        own[:, pl.ds(pl.multiple_of(PTS + block * LANES, LANES), LANES)] = got[1]
        return carry

    lax.fori_loop(0, PTS // LANES, gather, 0)

    own[:, AT_PROXY : AT_PROXY + RANKS] = jnp.zeros((8, RANKS), jnp.float32)
    for g in range(OWN):
        at = AT_PROXY + g * RANK
        own[0:3, at : at + RANK] = leaf_proxy[:, g, :] * SCALE

    first_half = lax.broadcasted_iota(jnp.int32, (NRHS, LANES), 1) < RANK
    parent = jnp.zeros((NRHS, RANK), jnp.float32)
    for m in range(OWN // 2):
        a = own[:, 2 * m * LEAF : (2 * m + 1) * LEAF].astype(jnp.bfloat16)
        b = own[:, (2 * m + 1) * LEAF : (2 * m + 2) * LEAF].astype(jnp.bfloat16)
        weights = jnp.reshape(basis[2 * m : 2 * m + 2], (2 * RANK, LEAF))
        pair = dot(jnp.concatenate([a, b], axis=0), weights, NT)
        coeffs = jnp.where(first_half, pair[:NRHS], pair[NRHS:])
        own[:, AT_COEFFS + m * LANES : AT_COEFFS + (m + 1) * LANES] = coeffs
        parent += dot3(coeffs, jnp.reshape(transfer[2 * m : 2 * m + 2], (2 * RANK, RANK)))

    entry[...] = jnp.zeros((NRHS, LANES), jnp.float32)
    entry[:, 0:RANK] = parent
    entry[0:3, RANK : 2 * RANK] = cluster_proxy[:, 0, :] * SCALE

    at = 0
    for start, whole, width in (
        (AT_CHARGES, PTS, NEAR_W), (AT_POINTS, PTS, NEAR_W),
        (AT_COEFFS, RANKS, FAR_W), (AT_PROXY, RANKS, FAR_W),
    ):
        left[:, at : at + width] = own[:, start : start + width]
        right[:, at : at + width] = own[:, start + whole - width : start + whole]
        at += width


def block_values(columns, rows):
    d0 = columns[0] - rows[0]
    d1 = columns[1] - rows[1]
    d2 = columns[2] - rows[2]
    return lax.rsqrt(d0 * d0 + d1 * d1 + d2 * d2 + SHIFT)


def product_kernel(
    near, far_cluster, far_leaf, own, from_left, from_right, table, cluster_proxy, transfer, basis,
    out,
    charges, points, coeffs, proxies, point_columns, proxy_columns, block, leaf_block, total, down,
    far_rows,
):
    group, member = lax.axis_index("leaf"), lax.axis_index("sub")
    cluster = group * NSUB + member
    first = cluster * OWN

    at = 0
    for window, start, whole, width in (
        (charges, AT_CHARGES, PTS, NEAR_W), (points, AT_POINTS, PTS, NEAR_W),
        (coeffs, AT_COEFFS, RANKS, FAR_W), (proxies, AT_PROXY, RANKS, FAR_W),
    ):
        window[:, 0:width] = from_left[:, at : at + width].astype(window.dtype)
        window[:, width : width + whole] = own[:, start : start + whole].astype(window.dtype)
        window[:, width + whole : 2 * width + whole] = from_right[:, at : at + width].astype(window.dtype)
        at += width
    for t in range(points.shape[1] // LANES):
        point_columns[t * LANES : (t + 1) * LANES, :] = points[:, t * LANES : (t + 1) * LANES].T
    for t in range(proxies.shape[1] // LANES):
        proxy_columns[t * LANES : (t + 1) * LANES, :] = proxies[:, t * LANES : (t + 1) * LANES].T

    total[...] = jnp.zeros_like(total)

    def listed(target, h):
        hit = near[0, target] == first + h
        for slot in range(1, near.shape[0]):
            hit = jnp.logical_or(hit, near[slot, target] == first + h)
        return hit.astype(jnp.float32)

    def strip(h, rows_at, lanes_at, width):
        rows = [points[c : c + 1, pl.ds(lanes_at, width)] for c in range(3)]
        step = 16
        for r in range(0, LEAF, step):
            column = point_columns[pl.ds(rows_at + r, step), :]
            values = block_values([column[:, c : c + 1] for c in range(3)], rows)
            block[r : r + step, 0:width] = values.astype(jnp.bfloat16)

    def near_leaf(h, carry):
        here = pl.multiple_of((h + REACH) * LEAF, LEAF)
        strip(h, here, here, (REACH + 1) * LEAF)
        forward = dot(charges[:, pl.ds(here, LEAF)], block[...])
        reverse = forward[:, 0:LEAF] * listed(h, h)
        for d in range(1, REACH + 1):
            there = pl.multiple_of((h + d + REACH) * LEAF, LEAF)
            lanes = slice(d * LEAF, (d + 1) * LEAF)
            total[:, pl.ds(there, LEAF)] += forward[:, lanes] * listed(jnp.minimum(h + d, OWN - 1), h)
            reverse += dot(charges[:, pl.ds(there, LEAF)], block[:, lanes], NT) * listed(h, h + d)
        total[:, pl.ds(here, LEAF)] += reverse
        return carry

    lax.fori_loop(0, OWN, near_leaf, 0)
    for h in range(-REACH, 0):
        width = (h + REACH + 1) * LEAF
        strip(h, (h + REACH) * LEAF, REACH * LEAF, width)
        forward = dot(charges[:, (h + REACH) * LEAF : (h + REACH + 1) * LEAF], block[:, 0:width])
        for g in range(h + REACH + 1):
            total[:, (g + REACH) * LEAF : (g + REACH + 1) * LEAF] += (
                forward[:, g * LEAF : (g + 1) * LEAF] * listed(g, h)
            )

    span = 3 * LANES
    first_lanes = lax.broadcasted_iota(jnp.int32, (NRHS, LANES), 1) < RANK
    down[...] = jnp.zeros_like(down)
    lists = far_leaf[...] - first + FREACH
    lists = jnp.where(far_leaf[...] >= 0, lists, -1)
    far_rows[...] = jnp.full_like(far_rows, -1)
    for m in range(OWN // 2):
        at = FAR_W + m * LANES
        far_rows[:, at : at + LANES] = jnp.where(
            first_lanes,
            jnp.broadcast_to(lists[:, 2 * m : 2 * m + 1], (8, LANES)),
            jnp.broadcast_to(lists[:, 2 * m + 1 : 2 * m + 2], (8, LANES)),
        )
    lane_leaf = lax.broadcasted_iota(jnp.int32, (8, span), 1) // RANK
    for m in range((FREACH + OWN) // 2):
        at = m * LANES
        to = at + LANES
        rows = [proxies[c : c + 1, to : to + span] for c in range(3)]
        for r in range(0, LANES, 32):
            column = proxy_columns[at + r : at + r + 32, :]
            leaf_block[r : r + 32, :] = block_values([column[:, c : c + 1] for c in range(3)], rows)
        high, low = split(leaf_block[...])
        pair = coeffs[:, at : at + LANES]
        sources = jnp.concatenate(
            [jnp.where(first_lanes, pair, 0.0), jnp.where(first_lanes, 0.0, pair)], axis=0
        )
        s_high, s_low = split(sources)
        both = dot(jnp.concatenate([s_high, s_low], axis=0), high)
        forward = both[:16] + both[16:] + dot(s_high, low)
        for i in range(2):
            hit = jnp.max((far_rows[:, to : to + span] == 2 * m + i).astype(jnp.float32), axis=0, keepdims=True)
            down[:, to : to + span] += forward[8 * i : 8 * i + 8] * hit
        if 2 * m >= FREACH:
            targets = coeffs[:, to : to + span]
            masked = []
            for i in range(2):
                column = lists[:, 2 * m + i - FREACH : 2 * m + i - FREACH + 1]
                hit = jnp.max((lane_leaf + (2 * m + 2) == column).astype(jnp.float32), axis=0, keepdims=True)
                masked.append(targets * hit)
            t_high, t_low = split(jnp.concatenate(masked, axis=0))
            both = dot(jnp.concatenate([t_high, t_low], axis=0), high, NT)
            reverse = both[:16] + both[16:] + dot(t_high, low, NT)
            down[:, at : at + LANES] += jnp.where(first_lanes, reverse[:8], reverse[8:])

    plane = group // PLANE
    entries, kept = [], []
    for slot in range(far_cluster.shape[1]):
        f = far_cluster[0, slot]
        valid = f >= 0
        f = jnp.where(valid, f, cluster)
        mine = f // (PLANE * NSUB) == plane
        place = lax.rem(f + jnp.where(mine, 0, HALF * NSUB), PLANE * NSUB)
        row = pl.multiple_of(jnp.where(mine, 0, NRHS), NRHS)
        e = table[place, pl.ds(row, NRHS), :]
        entries.append(e)
        kept.append(e * valid.astype(jnp.float32))
    parents, sources = [], []
    for m in range(len(entries) // 2):
        a, b = 2 * m, 2 * m + 1
        parents.append(jnp.where(first_lanes, kept[a], pltpu.roll(kept[b], RANK, 1)))
        sources.append(jnp.where(first_lanes, pltpu.roll(entries[a], RANK, 1), entries[b]))
    parents = jnp.concatenate(parents, axis=1)
    sources = jnp.concatenate(sources, axis=1)
    mine = jnp.concatenate([cluster_proxy[:, 0, :] * SCALE, jnp.zeros((5, RANK), jnp.float32)], axis=0)
    mine = jnp.concatenate([mine, mine], axis=1).T[:RANK]
    values = block_values(
        [mine[:, c : c + 1] for c in range(3)], [sources[c : c + 1, :] for c in range(3)]
    )
    coupled = dot3(parents, values, NT)

    for m in range(OWN // 2):
        weights = jnp.reshape(transfer[2 * m : 2 * m + 2], (2 * RANK, RANK))
        at = FAR_W + m * LANES
        pair = down[:, at : at + LANES] + dot3(coupled, weights, NT)
        d_high, d_low = split(
            jnp.concatenate([jnp.where(first_lanes, pair, 0.0), jnp.where(first_lanes, 0.0, pair)], axis=0)
        )
        both = dot(
            jnp.concatenate([d_high, d_low], axis=0), jnp.reshape(basis[2 * m : 2 * m + 2], (2 * RANK, LEAF))
        )
        far = both[:16] + both[16:]
        for i in range(2):
            at = (2 * m + i) * LEAF
            out[:, at : at + LEAF] = total[:, NEAR_W + at : NEAR_W + at + LEAF] + far[8 * i : 8 * i + 8]


def shards(
    points, charges, order, basis, transfer, leaf_proxy, cluster_proxy, near, far_leaf, far_cluster
):
    vmem = pl.BlockSpec(memory_space=pltpu.VMEM)
    smem = pl.BlockSpec(memory_space=pltpu.SMEM)
    f32 = jnp.float32
    leaf_proxy = leaf_proxy.transpose(1, 0, 2)
    cluster_proxy = cluster_proxy.transpose(1, 0, 2)
    own, right, left, entry = pl.pallas_call(
        prepare_kernel,
        in_specs=[vmem] * 7,
        out_specs=[vmem] * 4,
        out_shape=[
            jax.ShapeDtypeStruct((8, OWN_W), f32),
            jax.ShapeDtypeStruct((8, MSG), f32),
            jax.ShapeDtypeStruct((8, MSG), f32),
            jax.ShapeDtypeStruct((NRHS, LANES), f32),
        ],
        scratch_shapes=[pltpu.VMEM((2 * NRHS, PTS), f32)],
        compiler_params=pltpu.CompilerParams(vmem_limit_bytes=32 * 2**20),
        name="prepare",
    )(charges, points, order.reshape(PTS // LANES, LANES), basis, transfer, leaf_proxy, cluster_proxy)

    axes = ("leaf", "sub")
    groups, count = lax.axis_size("leaf"), lax.axis_size(axes)
    swap = []
    for start in range(HALF, groups - HALF, PLANE):
        for i in range(HALF):
            swap += [(start + i, start + HALF + i), (start + HALF + i, start + i)]
    partner = lax.ppermute(entry, "leaf", swap)
    from_left = lax.ppermute(right, axes, [(i, i + 1) for i in range(count - 1)])
    from_right = lax.ppermute(left, axes, [(i + 1, i) for i in range(count - 1)])
    size = PLANE * NSUB
    table = lax.all_to_all(
        jnp.broadcast_to(jnp.concatenate([entry, partner], axis=0), (size, 2 * NRHS, LANES)),
        axes, 0, 0, tiled=True,
        axis_index_groups=[list(range(i, i + size)) for i in range(0, count, size)],
    )

    window = OWN + 2 * REACH
    far_window = OWN + 2 * FREACH
    return pl.pallas_call(
        product_kernel,
        in_specs=[smem, smem] + [vmem] * 8,
        out_specs=vmem,
        out_shape=jax.ShapeDtypeStruct((NRHS, PTS), f32),
        scratch_shapes=[
            pltpu.VMEM((8, window * LEAF), jnp.bfloat16),
            pltpu.VMEM((8, window * LEAF), f32),
            pltpu.VMEM((8, far_window * RANK), f32),
            pltpu.VMEM((8, far_window * RANK), f32),
            pltpu.VMEM((window * LEAF, 8), f32),
            pltpu.VMEM((far_window * RANK, 8), f32),
            pltpu.VMEM((LEAF, (REACH + 1) * LEAF), jnp.bfloat16),
            pltpu.VMEM((2 * RANK, 3 * LANES), f32),
            pltpu.VMEM((NRHS, window * LEAF), f32),
            pltpu.VMEM((NRHS, far_window * RANK), f32),
            pltpu.VMEM((8, far_window * RANK), jnp.int32),
        ],
        compiler_params=pltpu.CompilerParams(vmem_limit_bytes=32 * 2**20),
        name="product",
    )(
        near.transpose(1, 0), far_cluster, far_leaf.transpose(1, 0), own, from_left, from_right, table,
        cluster_proxy, transfer, basis,
    )


def solution(mesh):
    in_specs = (
        P(None, ("leaf", "sub")),
        P(None, ("leaf", "sub")),
        P(("leaf", "sub")),
        P(("leaf", "sub"), None, None),
        P(("leaf", "sub"), None, None),
        P(("leaf", "sub"), None, None),
        P(("leaf", "sub"), None, None),
        P(("leaf", "sub"), None),
        P(("leaf", "sub"), None),
        P(("leaf", "sub"), None),
    )
    out_specs = P(None, ("leaf", "sub"))
    return jax.shard_map(shards, mesh=mesh, in_specs=in_specs, out_specs=out_specs, check_vma=False)
```

```python
import jax
import jax.numpy as jnp
from jax import lax
from jax.experimental import pallas as pl
from jax.experimental.pallas import tpu as pltpu
from jax.sharding import PartitionSpec as P

LEAF = 256
RANK = 64
NRHS = 8
OWN = 16
REACH = 2
FREACH = 6
PLANE = 8
HALF = PLANE // 2
NSUB = 4
PTS = OWN * LEAF
RANKS = OWN * RANK
LANES = 128
SCALE = 16.0
SHIFT = 2.56

NEAR_W = REACH * LEAF
FAR_W = FREACH * RANK
MSG = 2 * NEAR_W + 2 * FAR_W
AT_CHARGES, AT_POINTS, AT_COEFFS, AT_PROXY = 0, PTS, 2 * PTS, 2 * PTS + RANKS
OWN_W = 2 * PTS + 2 * RANKS

NT = (((1,), (1,)), ((), ()))
NN = (((1,), (0,)), ((), ()))


def dot(a, b, dims=NN):
    return lax.dot_general(a, b, dims, preferred_element_type=jnp.float32)


def split(x):
    high = x.astype(jnp.bfloat16)
    return high, (x - high.astype(jnp.float32)).astype(jnp.bfloat16)


def dot3(a, b, dims=NN):
    rows = a.shape[0]
    a_high, a_low = split(a)
    b_high, b_low = split(b)
    both = dot(jnp.concatenate([a_high, a_low], axis=0), b_high, dims)
    return both[:rows] + both[rows:] + dot(a_high, b_low, dims)


def prepare_kernel(
    charges, points, order, basis, transfer, leaf_proxy, cluster_proxy,
    own, right, left, spread,
    source, entry, charges_in, points_in, order_in, basis_in, transfer_in, leaf_proxy_in, cluster_proxy_in, sems,
):
    copies = [
        pltpu.make_async_copy(a, b, sems.at[i])
        for i, (a, b) in enumerate(
            (
                (order, order_in), (charges, charges_in), (points, points_in), (leaf_proxy, leaf_proxy_in),
                (cluster_proxy, cluster_proxy_in), (basis, basis_in), (transfer, transfer_in),
            )
        )
    ]
    for copy in copies:
        copy.start()
    own[:, AT_PROXY : AT_PROXY + RANKS] = jnp.zeros((8, RANKS), jnp.float32)
    entry[...] = jnp.zeros((NRHS, LANES), jnp.float32)
    source[NRHS : 2 * NRHS, :] = jnp.zeros((NRHS, PTS), jnp.float32)
    for copy in copies[:3]:
        copy.wait()
    source[0:NRHS, :] = charges_in[...].astype(jnp.float32)
    source[NRHS : NRHS + 3, :] = points_in[...] * SCALE

    def gather(block, carry):
        index = jnp.broadcast_to(order_in[pl.ds(block, 1), :], (8, LANES))
        high = lax.shift_right_logical(index, 7)
        low = jnp.bitwise_and(index, LANES - 1)
        lanes = pl.ds(pl.multiple_of(block * LANES, LANES), LANES)
        got = [None, None]
        for k in range(PTS // LANES):
            here = high == k
            for part in range(2):
                piece = source[8 * part : 8 * part + 8, k * LANES : (k + 1) * LANES]
                piece = jnp.take_along_axis(piece, low, axis=1)
                got[part] = piece if k == 0 else jnp.where(here, piece, got[part])
        own[:, lanes] = got[0]
        own[:, pl.ds(pl.multiple_of(PTS + block * LANES, LANES), LANES)] = got[1]
        return carry

    lax.fori_loop(0, PTS // LANES, gather, 0)

    for copy in copies[3:]:
        copy.wait()
    for g in range(OWN):
        at = AT_PROXY + g * RANK
        own[0:3, at : at + RANK] = leaf_proxy_in[:, g, :] * SCALE

    first_half = lax.broadcasted_iota(jnp.int32, (NRHS, LANES), 1) < RANK
    parent = jnp.zeros((NRHS, RANK), jnp.float32)
    for m in range(OWN // 2):
        a = own[:, 2 * m * LEAF : (2 * m + 1) * LEAF].astype(jnp.bfloat16)
        b = own[:, (2 * m + 1) * LEAF : (2 * m + 2) * LEAF].astype(jnp.bfloat16)
        weights = jnp.reshape(basis_in[2 * m : 2 * m + 2], (2 * RANK, LEAF))
        pair = dot(jnp.concatenate([a, b], axis=0), weights, NT)
        coeffs = jnp.where(first_half, pair[:NRHS], pair[NRHS:])
        own[:, AT_COEFFS + m * LANES : AT_COEFFS + (m + 1) * LANES] = coeffs
        parent += dot3(coeffs, jnp.reshape(transfer_in[2 * m : 2 * m + 2], (2 * RANK, RANK)))

    entry[:, 0:RANK] = parent
    entry[0:3, RANK : 2 * RANK] = cluster_proxy_in[:, 0, :] * SCALE

    for place in range(PLANE * NSUB):
        spread[place] = entry[...]

    at = 0
    for start, whole, width in (
        (AT_CHARGES, PTS, NEAR_W), (AT_POINTS, PTS, NEAR_W),
        (AT_COEFFS, RANKS, FAR_W), (AT_PROXY, RANKS, FAR_W),
    ):
        left[:, at : at + width] = own[:, start : start + width]
        right[:, at : at + width] = own[:, start + whole - width : start + whole]
        at += width


def block_values(columns, rows):
    d0 = columns[0] - rows[0]
    d1 = columns[1] - rows[1]
    d2 = columns[2] - rows[2]
    return lax.rsqrt(d0 * d0 + d1 * d1 + d2 * d2 + SHIFT)


def strip(columns, rows, block):
    step = 16
    for r in range(0, LEAF, step):
        column = columns[r : r + step, :]
        values = block_values([column[:, c : c + 1] for c in range(3)], rows)
        block[r : r + step, 0 : values.shape[1]] = values.astype(jnp.bfloat16)


def listing(near, first):
    def listed(target, h):
        hit = near[0, target] == first + h
        for slot in range(1, near.shape[0]):
            hit = jnp.logical_or(hit, near[slot, target] == first + h)
        return hit.astype(jnp.float32)

    return listed


def near_kernel(near_list, own, total, charges, columns, block, near, sem):
    copy = pltpu.make_async_copy(near_list, near, sem)
    copy.start()
    first = (lax.axis_index("leaf") * NSUB + lax.axis_index("sub")) * OWN
    listed = listing(near, first)
    charges[...] = own[:, 0:PTS].astype(jnp.bfloat16)
    for t in range(PTS // LANES):
        columns[t * LANES : (t + 1) * LANES, :] = own[:, PTS + t * LANES : PTS + (t + 1) * LANES].T
    total[...] = jnp.zeros_like(total)
    copy.wait()

    def leaf(h, reach, block):
        here = h * LEAF
        if not isinstance(h, int):
            here = pl.multiple_of(here, LEAF)
        lanes_at = PTS + here
        if not isinstance(h, int):
            lanes_at = pl.multiple_of(lanes_at, LEAF)
        rows = [own[c : c + 1, pl.ds(lanes_at, (reach + 1) * LEAF)] for c in range(3)]
        strip(columns.at[pl.ds(here, LEAF), :], rows, block)
        forward = dot(charges[:, pl.ds(here, LEAF)], block[:, 0 : (reach + 1) * LEAF])
        reverse = forward[:, 0:LEAF] * listed(h, h)
        for d in range(1, reach + 1):
            there = (h + d) * LEAF
            if not isinstance(h, int):
                there = pl.multiple_of(there, LEAF)
            lanes = slice(d * LEAF, (d + 1) * LEAF)
            total[:, pl.ds(there, LEAF)] += forward[:, lanes] * listed(h + d, h)
            reverse += dot(charges[:, pl.ds(there, LEAF)], block[:, lanes], NT) * listed(h, h + d)
        total[:, pl.ds(here, LEAF)] += reverse

    def pair(i, carry):
        for k in range(2):
            leaf(2 * i + k, REACH, block.at[k])
        return carry

    lax.fori_loop(0, (OWN - REACH) // 2, pair, 0)
    for h in range(OWN - REACH, OWN):
        leaf(h, OWN - 1 - h, block.at[h % 2])


def product_kernel(
    near_list, leaf_list, cluster_list, cluster_proxy_list, transfer, basis,
    own, from_left, from_right, total, table, beyond,
    out,
    coeffs, proxies, edge_columns, proxy_columns, block, leaf_block, down, far_rows,
    near, far_leaf, far_cluster, cluster_proxy, transfer_in, basis_in, sems,
):
    copies = [
        pltpu.make_async_copy(a, b, sems.at[i])
        for i, (a, b) in enumerate(
            (
                (near_list, near), (leaf_list, far_leaf), (cluster_list, far_cluster),
                (cluster_proxy_list, cluster_proxy), (transfer, transfer_in), (basis, basis_in),
            )
        )
    ]
    for copy in copies:
        copy.start()
    group = lax.axis_index("leaf")
    cluster = group * NSUB + lax.axis_index("sub")
    first = cluster * OWN

    at = 2 * NEAR_W
    for window, start, whole, width in (
        (coeffs, AT_COEFFS, RANKS, FAR_W), (proxies, AT_PROXY, RANKS, FAR_W),
    ):
        window[:, 0:width] = from_left[:, at : at + width]
        window[:, width : width + whole] = own[:, start : start + whole]
        window[:, width + whole : 2 * width + whole] = from_right[:, at : at + width]
        at += width
    for t in range(proxies.shape[1] // LANES):
        proxy_columns[t * LANES : (t + 1) * LANES, :] = proxies[:, t * LANES : (t + 1) * LANES].T

    for copy in copies[:4]:
        copy.wait()
    listed = listing(near, first)
    out[...] = total[...]
    for side, message in enumerate((from_left, from_right)):
        for t in range(NEAR_W // LANES):
            edge_columns[t * LANES : (t + 1) * LANES, :] = message[
                :, NEAR_W + t * LANES : NEAR_W + (t + 1) * LANES
            ].T
        for i in range(REACH):
            h = i - REACH if side == 0 else OWN + i
            targets = [g for g in range(OWN) if abs(g - h) <= REACH]
            at, width = targets[0] * LEAF, len(targets) * LEAF
            rows = [own[c : c + 1, PTS + at : PTS + at + width] for c in range(3)]
            strip(edge_columns.at[i * LEAF : (i + 1) * LEAF, :], rows, block.at[i])
            sources = message[:, i * LEAF : (i + 1) * LEAF].astype(jnp.bfloat16)
            forward = dot(sources, block[i, :, 0:width])
            for k, g in enumerate(targets):
                out[:, g * LEAF : (g + 1) * LEAF] += forward[:, k * LEAF : (k + 1) * LEAF] * listed(g, h)

    span = 3 * LANES
    first_lanes = lax.broadcasted_iota(jnp.int32, (NRHS, LANES), 1) < RANK
    down[...] = jnp.zeros_like(down)
    lists = far_leaf[...] - first + FREACH
    lists = jnp.where(far_leaf[...] >= 0, lists, -1)
    far_rows[...] = jnp.full_like(far_rows, -1)
    for m in range(OWN // 2):
        at = FAR_W + m * LANES
        far_rows[:, at : at + LANES] = jnp.where(
            first_lanes,
            jnp.broadcast_to(lists[:, 2 * m : 2 * m + 1], (8, LANES)),
            jnp.broadcast_to(lists[:, 2 * m + 1 : 2 * m + 2], (8, LANES)),
        )
    lane_leaf = lax.broadcasted_iota(jnp.int32, (8, span), 1) // RANK
    for m in range((FREACH + OWN) // 2):
        at = m * LANES
        to = at + LANES
        rows = [proxies[c : c + 1, to : to + span] for c in range(3)]
        for r in range(0, LANES, 32):
            column = proxy_columns[at + r : at + r + 32, :]
            leaf_block[r : r + 32, :] = block_values([column[:, c : c + 1] for c in range(3)], rows)
        high, low = split(leaf_block[...])
        pair = coeffs[:, at : at + LANES]
        sources = jnp.concatenate(
            [jnp.where(first_lanes, pair, 0.0), jnp.where(first_lanes, 0.0, pair)], axis=0
        )
        s_high, s_low = split(sources)
        both = dot(jnp.concatenate([s_high, s_low], axis=0), high)
        forward = both[:16] + both[16:] + dot(s_high, low)
        for i in range(2):
            hit = jnp.max((far_rows[:, to : to + span] == 2 * m + i).astype(jnp.float32), axis=0, keepdims=True)
            down[:, to : to + span] += forward[8 * i : 8 * i + 8] * hit
        if 2 * m >= FREACH:
            targets = coeffs[:, to : to + span]
            masked = []
            for i in range(2):
                column = lists[:, 2 * m + i - FREACH : 2 * m + i - FREACH + 1]
                hit = jnp.max((lane_leaf + (2 * m + 2) == column).astype(jnp.float32), axis=0, keepdims=True)
                masked.append(targets * hit)
            t_high, t_low = split(jnp.concatenate(masked, axis=0))
            both = dot(jnp.concatenate([t_high, t_low], axis=0), high, NT)
            reverse = both[:16] + both[16:] + dot(t_high, low, NT)
            down[:, at : at + LANES] += jnp.where(first_lanes, reverse[:8], reverse[8:])

    plane = group // PLANE
    entries, kept = [], []
    for slot in range(far_cluster.shape[1]):
        f = far_cluster[0, slot]
        valid = f >= 0
        f = jnp.where(valid, f, cluster)
        mine = f // (PLANE * NSUB) == plane
        place = lax.rem(f, PLANE * NSUB)
        e = jnp.where(mine, table[place], beyond[place])
        entries.append(e)
        kept.append(e * valid.astype(jnp.float32))
    parents, sources = [], []
    for m in range(len(entries) // 2):
        a, b = 2 * m, 2 * m + 1
        parents.append(jnp.where(first_lanes, kept[a], pltpu.roll(kept[b], RANK, 1)))
        sources.append(jnp.where(first_lanes, pltpu.roll(entries[a], RANK, 1), entries[b]))
    parents = jnp.concatenate(parents, axis=1)
    sources = jnp.concatenate(sources, axis=1)
    mine = jnp.concatenate([cluster_proxy[:, 0, :] * SCALE, jnp.zeros((5, RANK), jnp.float32)], axis=0)
    mine = jnp.concatenate([mine, mine], axis=1).T[:RANK]
    values = block_values(
        [mine[:, c : c + 1] for c in range(3)], [sources[c : c + 1, :] for c in range(3)]
    )
    coupled = dot3(parents, values, NT)

    for copy in copies[4:]:
        copy.wait()
    for m in range(OWN // 2):
        weights = jnp.reshape(transfer_in[2 * m : 2 * m + 2], (2 * RANK, RANK))
        at = FAR_W + m * LANES
        pair = down[:, at : at + LANES] + dot3(coupled, weights, NT)
        d_high, d_low = split(
            jnp.concatenate([jnp.where(first_lanes, pair, 0.0), jnp.where(first_lanes, 0.0, pair)], axis=0)
        )
        both = dot(
            jnp.concatenate([d_high, d_low], axis=0), jnp.reshape(basis_in[2 * m : 2 * m + 2], (2 * RANK, LEAF))
        )
        far = both[:16] + both[16:]
        for i in range(2):
            at = (2 * m + i) * LEAF
            out[:, at : at + LEAF] += far[8 * i : 8 * i + 8]


def shards(
    points, charges, order, basis, transfer, leaf_proxy, cluster_proxy, near, far_leaf, far_cluster
):
    vmem = pl.BlockSpec(memory_space=pltpu.VMEM)
    smem = pl.BlockSpec(memory_space=pltpu.SMEM)
    hbm = pl.BlockSpec(memory_space=pltpu.HBM)
    params = pltpu.CompilerParams(vmem_limit_bytes=48 * 2**20)
    f32 = jnp.float32
    leaf_proxy = leaf_proxy.transpose(1, 0, 2)
    cluster_proxy = cluster_proxy.transpose(1, 0, 2)
    near, far_leaf = near.transpose(1, 0), far_leaf.transpose(1, 0)
    given = (charges, points, order.reshape(PTS // LANES, LANES), basis, transfer, leaf_proxy, cluster_proxy)
    size = PLANE * NSUB
    own, right, left, spread = pl.pallas_call(
        prepare_kernel,
        in_specs=[hbm] * 7,
        out_specs=[vmem] * 4,
        out_shape=[
            jax.ShapeDtypeStruct((8, OWN_W), f32),
            jax.ShapeDtypeStruct((8, MSG), f32),
            jax.ShapeDtypeStruct((8, MSG), f32),
            jax.ShapeDtypeStruct((size, NRHS, LANES), f32),
        ],
        scratch_shapes=[pltpu.VMEM((2 * NRHS, PTS), f32), pltpu.VMEM((NRHS, LANES), f32)]
        + [pltpu.VMEM(a.shape, a.dtype) for a in given]
        + [pltpu.SemaphoreType.DMA((7,))],
        name="prepare",
    )(*given)

    axes = ("leaf", "sub")
    groups, count = lax.axis_size("leaf"), lax.axis_size(axes)
    table = lax.all_to_all(
        spread, axes, 0, 0, tiled=True,
        axis_index_groups=[list(range(i, i + size)) for i in range(0, count, size)],
    )
    from_left = lax.ppermute(right, axes, [(i, i + 1) for i in range(count - 1)])
    from_right = lax.ppermute(left, axes, [(i + 1, i) for i in range(count - 1)])
    shift = [(g - PLANE, g) for g in range(PLANE, groups) if g % PLANE < HALF]
    shift += [(g + PLANE, g) for g in range(groups - PLANE) if g % PLANE >= HALF]
    beyond = lax.ppermute(table, "leaf", shift)
    total = pl.pallas_call(
        near_kernel,
        in_specs=[hbm, vmem],
        out_specs=vmem,
        out_shape=jax.ShapeDtypeStruct((NRHS, PTS), f32),
        scratch_shapes=[
            pltpu.VMEM((8, PTS), jnp.bfloat16),
            pltpu.VMEM((PTS, 8), f32),
            pltpu.VMEM((2, LEAF, (REACH + 1) * LEAF), jnp.bfloat16),
            pltpu.SMEM(near.shape, near.dtype),
            pltpu.SemaphoreType.DMA,
        ],
        cost_estimate=pl.CostEstimate(flops=9 * 10**9, bytes_accessed=10**6, transcendentals=3 * 10**6),
        compiler_params=params,
        name="near_field",
    )(near, own)
    far_window = OWN + 2 * FREACH
    return pl.pallas_call(
        product_kernel,
        in_specs=[hbm] * 6 + [vmem] * 6,
        out_specs=vmem,
        out_shape=jax.ShapeDtypeStruct((NRHS, PTS), f32),
        scratch_shapes=[
            pltpu.VMEM((8, far_window * RANK), f32),
            pltpu.VMEM((8, far_window * RANK), f32),
            pltpu.VMEM((NEAR_W, 8), f32),
            pltpu.VMEM((far_window * RANK, 8), f32),
            pltpu.VMEM((REACH, LEAF, REACH * LEAF), jnp.bfloat16),
            pltpu.VMEM((2 * RANK, 3 * LANES), f32),
            pltpu.VMEM((8, far_window * RANK), f32),
            pltpu.VMEM((8, far_window * RANK), jnp.int32),
            pltpu.SMEM(near.shape, near.dtype),
            pltpu.VMEM(far_leaf.shape, far_leaf.dtype),
            pltpu.SMEM(far_cluster.shape, far_cluster.dtype),
            pltpu.VMEM(cluster_proxy.shape, cluster_proxy.dtype),
            pltpu.VMEM(transfer.shape, transfer.dtype),
            pltpu.VMEM(basis.shape, basis.dtype),
            pltpu.SemaphoreType.DMA((6,)),
        ],
        compiler_params=params,
        name="product",
    )(
        near, far_leaf, far_cluster, cluster_proxy, transfer, basis,
        own, from_left, from_right, total, table, beyond,
    )


def solution(mesh):
    in_specs = (
        P(None, ("leaf", "sub")),
        P(None, ("leaf", "sub")),
        P(("leaf", "sub")),
        P(("leaf", "sub"), None, None),
        P(("leaf", "sub"), None, None),
        P(("leaf", "sub"), None, None),
        P(("leaf", "sub"), None, None),
        P(("leaf", "sub"), None),
        P(("leaf", "sub"), None),
        P(("leaf", "sub"), None),
    )
    out_specs = P(None, ("leaf", "sub"))
    return jax.shard_map(shards, mesh=mesh, in_specs=in_specs, out_specs=out_specs, check_vma=False)
```

```python
import jax
import jax.numpy as jnp
from jax import lax
from jax.experimental import pallas as pl
from jax.experimental.pallas import tpu as pltpu
from jax.sharding import PartitionSpec as P

LEAF = 256
RANK = 64
NRHS = 8
OWN = 16
REACH = 2
FREACH = 6
PLANE = 8
HALF = PLANE // 2
NSUB = 4
PTS = OWN * LEAF
RANKS = OWN * RANK
LANES = 128
BUFFERS = 4
SCALE = 16.0
SHIFT = 2.56

NEAR_W = REACH * LEAF
FAR_W = FREACH * RANK
MSG = 2 * NEAR_W + 2 * FAR_W
AT_CHARGES, AT_POINTS, AT_COEFFS, AT_PROXY = 0, PTS, 2 * PTS, 2 * PTS + RANKS
OWN_W = 2 * PTS + 2 * RANKS

NT = (((1,), (1,)), ((), ()))
NN = (((1,), (0,)), ((), ()))


def dot(a, b, dims=NN):
    return lax.dot_general(a, b, dims, preferred_element_type=jnp.float32)


def split(x):
    high = x.astype(jnp.bfloat16)
    return high, (x - high.astype(jnp.float32)).astype(jnp.bfloat16)


def dot3(a, b, dims=NN):
    rows = a.shape[0]
    a_high, a_low = split(a)
    b_high, b_low = split(b)
    both = dot(jnp.concatenate([a_high, a_low], axis=0), b_high, dims)
    return both[:rows] + both[rows:] + dot(a_high, b_low, dims)


ALONG_LANES = lax.GatherDimensionNumbers(
    offset_dims=(), collapsed_slice_dims=(1,), start_index_map=(1,), operand_batching_dims=(0,),
    start_indices_batching_dims=(0,),
)


def picked(source, index, count, dtype):
    low = jnp.bitwise_and(index, dtype(LANES - 1))[..., None]
    bits, k = [], 1
    while k < count:
        bits.append(jnp.bitwise_and(index, dtype(k * LANES)) != 0)
        k *= 2

    def among(first, level):
        if level == 0:
            return lax.gather(
                source(first), low, ALONG_LANES, (1, 1), mode=lax.GatherScatterMode.PROMISE_IN_BOUNDS
            )
        size = 1 << (level - 1)
        return jnp.where(bits[level - 1], among(first + size, level - 1), among(first, level - 1))

    return among(0, len(bits))


def prepare_kernel(
    charges, points, order, basis, transfer, leaf_proxy, cluster_proxy,
    own, right, left, spread,
    twice, entry, charges_in, points_in, order_in, basis_in, transfer_in, leaf_proxy_in, cluster_proxy_in, sems,
):
    copies = [
        pltpu.make_async_copy(a, b, sems.at[i])
        for i, (a, b) in enumerate(
            (
                (order, order_in), (charges, charges_in), (points, points_in), (leaf_proxy, leaf_proxy_in),
                (cluster_proxy, cluster_proxy_in), (basis, basis_in), (transfer, transfer_in),
            )
        )
    ]
    for copy in copies:
        copy.start()
    own[:, AT_PROXY : AT_PROXY + RANKS] = jnp.zeros((8, RANKS), jnp.float32)
    entry[...] = jnp.zeros((NRHS, LANES), jnp.float32)
    own[:, AT_POINTS : AT_POINTS + PTS] = jnp.zeros((8, PTS), jnp.float32)
    for copy in copies[:3]:
        copy.wait()
    blocks = PTS // LANES
    both = charges_in[...].astype(jnp.float32)
    twice[...] = jnp.concatenate([both, both], axis=0).astype(jnp.bfloat16)

    for i in range(blocks // 2):
        index = jnp.concatenate(
            [jnp.broadcast_to(order_in[2 * i + k : 2 * i + k + 1, :], (NRHS, LANES)) for k in range(2)], axis=0
        ).astype(jnp.int16)
        got = picked(
            lambda k: twice[:, k * LANES : (k + 1) * LANES], index, blocks, jnp.int16
        ).astype(jnp.float32)
        for k in range(2):
            own[:, (2 * i + k) * LANES : (2 * i + k + 1) * LANES] = got[NRHS * k : NRHS * (k + 1)]

    for j in range(blocks // 8):
        index = order_in[8 * j : 8 * j + 8, :]
        for c in range(3):
            got = picked(
                lambda k: jnp.broadcast_to(points_in[c : c + 1, k * LANES : (k + 1) * LANES], (8, LANES)),
                index, blocks, jnp.int32,
            ) * SCALE
            for s in range(8):
                at = AT_POINTS + (8 * j + s) * LANES
                own[c : c + 1, at : at + LANES] = got[s : s + 1]

    for copy in copies[3:]:
        copy.wait()
    for g in range(OWN):
        at = AT_PROXY + g * RANK
        own[0:3, at : at + RANK] = leaf_proxy_in[:, g, :] * SCALE

    first_half = lax.broadcasted_iota(jnp.int32, (NRHS, LANES), 1) < RANK
    parent = jnp.zeros((NRHS, RANK), jnp.float32)
    for m in range(OWN // 2):
        a = own[:, 2 * m * LEAF : (2 * m + 1) * LEAF].astype(jnp.bfloat16)
        b = own[:, (2 * m + 1) * LEAF : (2 * m + 2) * LEAF].astype(jnp.bfloat16)
        weights = jnp.reshape(basis_in[2 * m : 2 * m + 2], (2 * RANK, LEAF))
        pair = dot(jnp.concatenate([a, b], axis=0), weights, NT)
        coeffs = jnp.where(first_half, pair[:NRHS], pair[NRHS:])
        own[:, AT_COEFFS + m * LANES : AT_COEFFS + (m + 1) * LANES] = coeffs
        parent += dot3(coeffs, jnp.reshape(transfer_in[2 * m : 2 * m + 2], (2 * RANK, RANK)))

    entry[:, 0:RANK] = parent
    entry[0:3, RANK : 2 * RANK] = cluster_proxy_in[:, 0, :] * SCALE

    for place in range(PLANE * NSUB):
        spread[place] = entry[...]

    at = 0
    for start, whole, width in (
        (AT_CHARGES, PTS, NEAR_W), (AT_POINTS, PTS, NEAR_W),
        (AT_COEFFS, RANKS, FAR_W), (AT_PROXY, RANKS, FAR_W),
    ):
        left[:, at : at + width] = own[:, start : start + width]
        right[:, at : at + width] = own[:, start + whole - width : start + whole]
        at += width


def block_values(columns, rows):
    d0 = columns[0] - rows[0]
    d1 = columns[1] - rows[1]
    d2 = columns[2] - rows[2]
    return lax.rsqrt(d0 * d0 + d1 * d1 + d2 * d2 + SHIFT)


def features(points, as_source):
    row = lax.broadcasted_iota(jnp.int32, points.shape, 0)
    h = jnp.floor(points * 2.0 + 0.5) * 0.5
    l = points - h
    l1 = l.astype(jnp.bfloat16).astype(jnp.float32)
    l2 = l - l1
    n = jnp.sum(h * h, axis=0, keepdims=True)
    n1 = jnp.floor(n * (1 / 128) + 0.5) * 128.0
    n2 = n - n1
    s = jnp.sum((2.0 * h + l) * l, axis=0, keepdims=True) + SHIFT / 2
    s1 = s.astype(jnp.bfloat16).astype(jnp.float32)
    s2 = (s - s1).astype(jnp.bfloat16).astype(jnp.float32)
    s3 = s - s1 - s2

    def stack(vector, *others):
        for i, other in enumerate(others):
            vector = jnp.where(row == 3 + i, other, vector)
        return vector

    if as_source:
        groups = [
            stack(h, n1, n2, 1.0, 1.0), stack(h, s1, s2, s3, 1.0, 1.0), stack(h, 1.0), l1, l2, l1, l1, l2
        ]
    else:
        h, l1, l2 = -2.0 * h, -2.0 * l1, -2.0 * l2
        groups = [
            stack(h, 1.0, 1.0, n1, n2), stack(l1, 1.0, 1.0, 1.0, s1, s2), stack(l2, s3), h, h, l1, l2, l1
        ]
    return jnp.concatenate(groups, axis=0).astype(jnp.bfloat16)


def strip(sources, targets, block):
    for at in range(0, targets.shape[1], LEAF):
        block[:, at : at + LEAF] = lax.rsqrt(dot(sources, targets[:, at : at + LEAF])).astype(jnp.bfloat16)


def listing(near, first):
    def listed(target, h):
        hit = near[0, target] == first + h
        for slot in range(1, near.shape[0]):
            hit = jnp.logical_or(hit, near[slot, target] == first + h)
        return hit.astype(jnp.float32)

    return listed


def near_kernel(near_list, own, total, charges, sources, targets, block, near, sem):
    copy = pltpu.make_async_copy(near_list, near, sem)
    copy.start()
    first = (lax.axis_index("leaf") * NSUB + lax.axis_index("sub")) * OWN
    listed = listing(near, first)
    charges[...] = own[:, 0:PTS].astype(jnp.bfloat16)
    for t in range(PTS // LANES):
        points = own[:, PTS + t * LANES : PTS + (t + 1) * LANES]
        sources[t * LANES : (t + 1) * LANES, :] = features(points, True).T
        targets[:, t * LANES : (t + 1) * LANES] = features(points, False)
    copy.wait()

    sums = [0.0] * OWN
    for step in range(OWN + 1):
        for d in range(REACH + 1):
            h = step
            if h + d < OWN:
                strip(
                    sources[h * LEAF : (h + 1) * LEAF, :],
                    targets[:, (h + d) * LEAF : (h + d + 1) * LEAF],
                    block.at[h % BUFFERS, d],
                )
            h = step - 1
            if h >= 0 and h + d < OWN:
                here = slice(h * LEAF, (h + 1) * LEAF)
                there = slice((h + d) * LEAF, (h + d + 1) * LEAF)
                values = block[h % BUFFERS, d]
                sums[h + d] += dot(charges[:, here], values) * listed(h + d, h)
                if d > 0:
                    sums[h] += dot(charges[:, there], values, NT) * listed(h, h + d)
        if step > 0:
            total[:, (step - 1) * LEAF : step * LEAF] = sums[step - 1]


def product_kernel(
    near_list, leaf_list, cluster_list, cluster_proxy_list, transfer, basis,
    own, from_left, from_right, total, table, beyond,
    out,
    coeffs, proxies, proxy_columns, block, leaf_block, down, far_rows,
    near, far_leaf, far_cluster, cluster_proxy, transfer_in, basis_in, sems,
):
    copies = [
        pltpu.make_async_copy(a, b, sems.at[i])
        for i, (a, b) in enumerate(
            (
                (near_list, near), (leaf_list, far_leaf), (cluster_list, far_cluster),
                (cluster_proxy_list, cluster_proxy), (transfer, transfer_in), (basis, basis_in),
            )
        )
    ]
    for copy in copies:
        copy.start()
    group = lax.axis_index("leaf")
    cluster = group * NSUB + lax.axis_index("sub")
    first = cluster * OWN

    at = 2 * NEAR_W
    for window, start, whole, width in (
        (coeffs, AT_COEFFS, RANKS, FAR_W), (proxies, AT_PROXY, RANKS, FAR_W),
    ):
        window[:, 0:width] = from_left[:, at : at + width]
        window[:, width : width + whole] = own[:, start : start + whole]
        window[:, width + whole : 2 * width + whole] = from_right[:, at : at + width]
        at += width
    for t in range(proxies.shape[1] // LANES):
        proxy_columns[t * LANES : (t + 1) * LANES, :] = proxies[:, t * LANES : (t + 1) * LANES].T

    for copy in copies[:4]:
        copy.wait()
    listed = listing(near, first)
    out[...] = total[...]
    for side, message in enumerate((from_left, from_right)):
        sources = features(message[:, NEAR_W : 2 * NEAR_W], True).T
        at = 0 if side == 0 else PTS - NEAR_W
        targets = features(own[:, PTS + at : PTS + at + NEAR_W], False)
        for i in range(REACH):
            h = i - REACH if side == 0 else OWN + i
            leaves = [g for g in range(OWN) if abs(g - h) <= REACH]
            width = len(leaves) * LEAF
            skip = leaves[0] * LEAF - at
            strip(sources[i * LEAF : (i + 1) * LEAF], targets[:, skip : skip + width], block.at[i])
            weights = message[:, i * LEAF : (i + 1) * LEAF].astype(jnp.bfloat16)
            forward = dot(weights, block[i, :, 0:width])
            for k, g in enumerate(leaves):
                out[:, g * LEAF : (g + 1) * LEAF] += forward[:, k * LEAF : (k + 1) * LEAF] * listed(g, h)

    span = 3 * LANES
    first_lanes = lax.broadcasted_iota(jnp.int32, (NRHS, LANES), 1) < RANK
    down[...] = jnp.zeros_like(down)
    lists = far_leaf[...] - first + FREACH
    lists = jnp.where(far_leaf[...] >= 0, lists, -1)
    far_rows[...] = jnp.full_like(far_rows, -1)
    for m in range(OWN // 2):
        at = FAR_W + m * LANES
        far_rows[:, at : at + LANES] = jnp.where(
            first_lanes,
            jnp.broadcast_to(lists[:, 2 * m : 2 * m + 1], (8, LANES)),
            jnp.broadcast_to(lists[:, 2 * m + 1 : 2 * m + 2], (8, LANES)),
        )
    lane_leaf = lax.broadcasted_iota(jnp.int32, (8, span), 1) // RANK
    for m in range((FREACH + OWN) // 2):
        at = m * LANES
        to = at + LANES
        rows = [proxies[c : c + 1, to : to + span] for c in range(3)]
        for r in range(0, LANES, 32):
            column = proxy_columns[at + r : at + r + 32, :]
            leaf_block[r : r + 32, :] = block_values([column[:, c : c + 1] for c in range(3)], rows)
        high, low = split(leaf_block[...])
        pair = coeffs[:, at : at + LANES]
        sources = jnp.concatenate(
            [jnp.where(first_lanes, pair, 0.0), jnp.where(first_lanes, 0.0, pair)], axis=0
        )
        s_high, s_low = split(sources)
        both = dot(jnp.concatenate([s_high, s_low], axis=0), high)
        forward = both[:16] + both[16:] + dot(s_high, low)
        for i in range(2):
            hit = jnp.max((far_rows[:, to : to + span] == 2 * m + i).astype(jnp.float32), axis=0, keepdims=True)
            down[:, to : to + span] += forward[8 * i : 8 * i + 8] * hit
        if 2 * m >= FREACH:
            targets = coeffs[:, to : to + span]
            masked = []
            for i in range(2):
                column = lists[:, 2 * m + i - FREACH : 2 * m + i - FREACH + 1]
                hit = jnp.max((lane_leaf + (2 * m + 2) == column).astype(jnp.float32), axis=0, keepdims=True)
                masked.append(targets * hit)
            t_high, t_low = split(jnp.concatenate(masked, axis=0))
            both = dot(jnp.concatenate([t_high, t_low], axis=0), high, NT)
            reverse = both[:16] + both[16:] + dot(t_high, low, NT)
            down[:, at : at + LANES] += jnp.where(first_lanes, reverse[:8], reverse[8:])

    plane = group // PLANE
    entries, kept = [], []
    for slot in range(far_cluster.shape[1]):
        f = far_cluster[0, slot]
        valid = f >= 0
        f = jnp.where(valid, f, cluster)
        mine = f // (PLANE * NSUB) == plane
        place = lax.rem(f, PLANE * NSUB)
        e = jnp.where(mine, table[place], beyond[place])
        entries.append(e)
        kept.append(e * valid.astype(jnp.float32))
    parents, sources = [], []
    for m in range(len(entries) // 2):
        a, b = 2 * m, 2 * m + 1
        parents.append(jnp.where(first_lanes, kept[a], pltpu.roll(kept[b], RANK, 1)))
        sources.append(jnp.where(first_lanes, pltpu.roll(entries[a], RANK, 1), entries[b]))
    parents = jnp.concatenate(parents, axis=1)
    sources = jnp.concatenate(sources, axis=1)
    mine = jnp.concatenate([cluster_proxy[:, 0, :] * SCALE, jnp.zeros((5, RANK), jnp.float32)], axis=0)
    mine = jnp.concatenate([mine, mine], axis=1).T[:RANK]
    values = block_values(
        [mine[:, c : c + 1] for c in range(3)], [sources[c : c + 1, :] for c in range(3)]
    )
    coupled = dot3(parents, values, NT)

    for copy in copies[4:]:
        copy.wait()
    for m in range(OWN // 2):
        weights = jnp.reshape(transfer_in[2 * m : 2 * m + 2], (2 * RANK, RANK))
        at = FAR_W + m * LANES
        pair = down[:, at : at + LANES] + dot3(coupled, weights, NT)
        d_high, d_low = split(
            jnp.concatenate([jnp.where(first_lanes, pair, 0.0), jnp.where(first_lanes, 0.0, pair)], axis=0)
        )
        both = dot(
            jnp.concatenate([d_high, d_low], axis=0), jnp.reshape(basis_in[2 * m : 2 * m + 2], (2 * RANK, LEAF))
        )
        far = both[:16] + both[16:]
        for i in range(2):
            at = (2 * m + i) * LEAF
            out[:, at : at + LEAF] += far[8 * i : 8 * i + 8]


def shards(
    points, charges, order, basis, transfer, leaf_proxy, cluster_proxy, near, far_leaf, far_cluster
):
    vmem = pl.BlockSpec(memory_space=pltpu.VMEM)
    smem = pl.BlockSpec(memory_space=pltpu.SMEM)
    hbm = pl.BlockSpec(memory_space=pltpu.HBM)
    params = pltpu.CompilerParams(vmem_limit_bytes=48 * 2**20)
    f32 = jnp.float32
    leaf_proxy = leaf_proxy.transpose(1, 0, 2)
    cluster_proxy = cluster_proxy.transpose(1, 0, 2)
    near, far_leaf = near.transpose(1, 0), far_leaf.transpose(1, 0)
    given = (charges, points, order.reshape(PTS // LANES, LANES), basis, transfer, leaf_proxy, cluster_proxy)
    size = PLANE * NSUB
    own, right, left, spread = pl.pallas_call(
        prepare_kernel,
        in_specs=[hbm] * 7,
        out_specs=[vmem] * 4,
        out_shape=[
            jax.ShapeDtypeStruct((8, OWN_W), f32),
            jax.ShapeDtypeStruct((8, MSG), f32),
            jax.ShapeDtypeStruct((8, MSG), f32),
            jax.ShapeDtypeStruct((size, NRHS, LANES), f32),
        ],
        scratch_shapes=[pltpu.VMEM((2 * NRHS, PTS), jnp.bfloat16), pltpu.VMEM((NRHS, LANES), f32)]
        + [pltpu.VMEM(a.shape, a.dtype) for a in given]
        + [pltpu.SemaphoreType.DMA((7,))],
        name="prepare",
    )(*given)

    axes = ("leaf", "sub")
    groups, count = lax.axis_size("leaf"), lax.axis_size(axes)
    table = lax.all_to_all(
        spread, axes, 0, 0, tiled=True,
        axis_index_groups=[list(range(i, i + size)) for i in range(0, count, size)],
    )
    from_left = lax.ppermute(right, axes, [(i, i + 1) for i in range(count - 1)])
    from_right = lax.ppermute(left, axes, [(i + 1, i) for i in range(count - 1)])
    shift = [(g - PLANE, g) for g in range(PLANE, groups) if g % PLANE < HALF]
    shift += [(g + PLANE, g) for g in range(groups - PLANE) if g % PLANE >= HALF]
    beyond = lax.ppermute(table, "leaf", shift)
    total = pl.pallas_call(
        near_kernel,
        in_specs=[hbm, vmem],
        out_specs=vmem,
        out_shape=jax.ShapeDtypeStruct((NRHS, PTS), f32),
        scratch_shapes=[
            pltpu.VMEM((8, PTS), jnp.bfloat16),
            pltpu.VMEM((PTS, 64), jnp.bfloat16),
            pltpu.VMEM((64, PTS), jnp.bfloat16),
            pltpu.VMEM((BUFFERS, REACH + 1, LEAF, LEAF), jnp.bfloat16),
            pltpu.SMEM(near.shape, near.dtype),
            pltpu.SemaphoreType.DMA,
        ],
        cost_estimate=pl.CostEstimate(flops=9 * 10**9, bytes_accessed=10**6, transcendentals=3 * 10**6),
        compiler_params=params,
        name="near_field",
    )(near, own)
    far_window = OWN + 2 * FREACH
    return pl.pallas_call(
        product_kernel,
        in_specs=[hbm] * 6 + [vmem] * 6,
        out_specs=vmem,
        out_shape=jax.ShapeDtypeStruct((NRHS, PTS), f32),
        scratch_shapes=[
            pltpu.VMEM((8, far_window * RANK), f32),
            pltpu.VMEM((8, far_window * RANK), f32),
            pltpu.VMEM((far_window * RANK, 8), f32),
            pltpu.VMEM((REACH, LEAF, REACH * LEAF), jnp.bfloat16),
            pltpu.VMEM((2 * RANK, 3 * LANES), f32),
            pltpu.VMEM((8, far_window * RANK), f32),
            pltpu.VMEM((8, far_window * RANK), jnp.int32),
            pltpu.SMEM(near.shape, near.dtype),
            pltpu.VMEM(far_leaf.shape, far_leaf.dtype),
            pltpu.SMEM(far_cluster.shape, far_cluster.dtype),
            pltpu.VMEM(cluster_proxy.shape, cluster_proxy.dtype),
            pltpu.VMEM(transfer.shape, transfer.dtype),
            pltpu.VMEM(basis.shape, basis.dtype),
            pltpu.SemaphoreType.DMA((6,)),
        ],
        compiler_params=params,
        name="product",
    )(
        near, far_leaf, far_cluster, cluster_proxy, transfer, basis,
        own, from_left, from_right, total, table, beyond,
    )


def solution(mesh):
    in_specs = (
        P(None, ("leaf", "sub")),
        P(None, ("leaf", "sub")),
        P(("leaf", "sub")),
        P(("leaf", "sub"), None, None),
        P(("leaf", "sub"), None, None),
        P(("leaf", "sub"), None, None),
        P(("leaf", "sub"), None, None),
        P(("leaf", "sub"), None),
        P(("leaf", "sub"), None),
        P(("leaf", "sub"), None),
    )
    out_specs = P(None, ("leaf", "sub"))
    return jax.shard_map(shards, mesh=mesh, in_specs=in_specs, out_specs=out_specs, check_vma=False)
```

```python
import jax
import jax.numpy as jnp
from jax import lax
from jax.experimental import pallas as pl
from jax.experimental.pallas import tpu as pltpu
from jax.sharding import PartitionSpec as P

LEAF = 256
RANK = 64
NRHS = 8
OWN = 16
REACH = 2
FREACH = 6
PLANE = 8
HALF = PLANE // 2
NSUB = 4
FAR1 = 16
PTS = OWN * LEAF
RANKS = OWN * RANK
LANES = 128
BUFFERS = 4
AHEAD = 2
SCALE = 16.0
SHIFT = 2.56

NEAR_W = REACH * LEAF
FAR_W = FREACH * RANK
MSG = 2 * NEAR_W + 2 * FAR_W
AT_CHARGES, AT_POINTS, AT_COEFFS, AT_PROXY = 0, PTS, 2 * PTS, 2 * PTS + RANKS
AT_LIST = 2 * PTS + 2 * RANKS
OWN_W = AT_LIST + LANES

NT = (((1,), (1,)), ((), ()))
NN = (((1,), (0,)), ((), ()))


def dot(a, b, dims=NN):
    return lax.dot_general(a, b, dims, preferred_element_type=jnp.float32)


def split(x):
    high = x.astype(jnp.bfloat16)
    return high, (x - high.astype(jnp.float32)).astype(jnp.bfloat16)


def dot3(a, b, dims=NN):
    rows = a.shape[0]
    a_high, a_low = split(a)
    b_high, b_low = split(b)
    both = dot(jnp.concatenate([a_high, a_low], axis=0), b_high, dims)
    return both[:rows] + both[rows:] + dot(a_high, b_low, dims)


ALONG_LANES = lax.GatherDimensionNumbers(
    offset_dims=(), collapsed_slice_dims=(1,), start_index_map=(1,), operand_batching_dims=(0,),
    start_indices_batching_dims=(0,),
)


def picked(source, index, count, dtype):
    low = jnp.bitwise_and(index, dtype(LANES - 1))[..., None]
    bits, k = [], 1
    while k < count:
        bits.append(jnp.bitwise_and(index, dtype(k * LANES)) != 0)
        k *= 2

    def among(first, level):
        if level == 0:
            return lax.gather(
                source(first), low, ALONG_LANES, (1, 1), mode=lax.GatherScatterMode.PROMISE_IN_BOUNDS
            )
        size = 1 << (level - 1)
        return jnp.where(bits[level - 1], among(first + size, level - 1), among(first, level - 1))

    return among(0, len(bits))


def prepare_kernel(
    charges, points, order, basis, transfer, leaf_proxy, cluster_proxy, far_cluster,
    own, right, left, spread,
    twice, entry, charges_in, points_in, order_in, basis_in, transfer_in, leaf_proxy_in, cluster_proxy_in, far_cluster_in, sems,
):
    copies = [
        pltpu.make_async_copy(a, b, sems.at[i])
        for i, (a, b) in enumerate(
            (
                (order, order_in), (charges, charges_in), (points, points_in), (leaf_proxy, leaf_proxy_in),
                (cluster_proxy, cluster_proxy_in), (far_cluster, far_cluster_in), (basis, basis_in),
                (transfer, transfer_in),
            )
        )
    ]
    for copy in copies:
        copy.start()
    own[:, AT_PROXY : AT_PROXY + RANKS] = jnp.zeros((8, RANKS), jnp.float32)
    entry[...] = jnp.zeros((NRHS, LANES), jnp.float32)
    own[:, AT_POINTS : AT_POINTS + PTS] = jnp.zeros((8, PTS), jnp.float32)
    for copy in copies[:3]:
        copy.wait()
    blocks = PTS // LANES
    both = charges_in[...].astype(jnp.float32)
    twice[...] = jnp.concatenate([both, both], axis=0).astype(jnp.bfloat16)

    for i in range(blocks // 2):
        index = jnp.concatenate(
            [jnp.broadcast_to(order_in[2 * i + k : 2 * i + k + 1, :], (NRHS, LANES)) for k in range(2)], axis=0
        ).astype(jnp.int16)
        got = picked(
            lambda k: twice[:, k * LANES : (k + 1) * LANES], index, blocks, jnp.int16
        ).astype(jnp.float32)
        for k in range(2):
            own[:, (2 * i + k) * LANES : (2 * i + k + 1) * LANES] = got[NRHS * k : NRHS * (k + 1)]

    for j in range(blocks // 8):
        index = order_in[8 * j : 8 * j + 8, :]
        for c in range(3):
            got = picked(
                lambda k: jnp.broadcast_to(points_in[c : c + 1, k * LANES : (k + 1) * LANES], (8, LANES)),
                index, blocks, jnp.int32,
            ) * SCALE
            for s in range(8):
                at = AT_POINTS + (8 * j + s) * LANES
                own[c : c + 1, at : at + LANES] = got[s : s + 1]

    for copy in copies[3:]:
        copy.wait()
    for g in range(OWN):
        at = AT_PROXY + g * RANK
        own[0:3, at : at + RANK] = leaf_proxy_in[:, g, :] * SCALE

    own[:, AT_LIST:] = jnp.zeros((8, LANES), jnp.float32)
    own[0:1, AT_LIST : AT_LIST + far_cluster_in.shape[1]] = far_cluster_in[...].astype(jnp.float32)

    first_half = lax.broadcasted_iota(jnp.int32, (NRHS, LANES), 1) < RANK
    parent = jnp.zeros((NRHS, RANK), jnp.float32)
    pairs = range(OWN // 2)
    both = [
        dot(
            jnp.concatenate(
                [own[:, g * LEAF : (g + 1) * LEAF].astype(jnp.bfloat16) for g in (2 * m, 2 * m + 1)], axis=0
            ),
            jnp.reshape(basis_in[2 * m : 2 * m + 2], (2 * RANK, LEAF)),
            NT,
        )
        for m in pairs
    ]
    coeffs = [jnp.where(first_half, both[m][:NRHS], both[m][NRHS:]) for m in pairs]
    for m in pairs:
        own[:, AT_COEFFS + m * LANES : AT_COEFFS + (m + 1) * LANES] = coeffs[m]
        parent += dot3(coeffs[m], jnp.reshape(transfer_in[2 * m : 2 * m + 2], (2 * RANK, RANK)))

    entry[:, 0:RANK] = parent
    entry[0:3, RANK : 2 * RANK] = cluster_proxy_in[:, 0, :] * SCALE

    for place in range(PLANE * NSUB):
        spread[place] = entry[...]

    at = 0
    for start, whole, width in (
        (AT_CHARGES, PTS, NEAR_W), (AT_POINTS, PTS, NEAR_W),
        (AT_COEFFS, RANKS, FAR_W), (AT_PROXY, RANKS, FAR_W),
    ):
        left[:, at : at + width] = own[:, start : start + width]
        right[:, at : at + width] = own[:, start + whole - width : start + whole]
        at += width


def block_values(columns, rows):
    d0 = columns[0] - rows[0]
    d1 = columns[1] - rows[1]
    d2 = columns[2] - rows[2]
    return lax.rsqrt(d0 * d0 + d1 * d1 + d2 * d2 + SHIFT)


def features(points, as_source):
    row = lax.broadcasted_iota(jnp.int32, points.shape, 0)
    h = jnp.floor(points * 2.0 + 0.5) * 0.5
    l = points - h
    l1 = l.astype(jnp.bfloat16).astype(jnp.float32)
    l2 = l - l1
    n = jnp.sum(h * h, axis=0, keepdims=True)
    n1 = jnp.floor(n * (1 / 128) + 0.5) * 128.0
    n2 = n - n1
    s = jnp.sum((2.0 * h + l) * l, axis=0, keepdims=True) + SHIFT / 2
    s1 = s.astype(jnp.bfloat16).astype(jnp.float32)
    s2 = (s - s1).astype(jnp.bfloat16).astype(jnp.float32)
    s3 = s - s1 - s2

    def stack(vector, *others):
        for i, other in enumerate(others):
            vector = jnp.where(row == 3 + i, other, vector)
        return vector

    if as_source:
        groups = [
            stack(h, n1, n2, 1.0, 1.0), stack(h, s1, s2, s3, 1.0, 1.0), stack(h, 1.0), l1, l2, l1, l1, l2
        ]
    else:
        h, l1, l2 = -2.0 * h, -2.0 * l1, -2.0 * l2
        groups = [
            stack(h, 1.0, 1.0, n1, n2), stack(l1, 1.0, 1.0, 1.0, s1, s2), stack(l2, s3), h, h, l1, l2, l1
        ]
    return jnp.concatenate(groups, axis=0).astype(jnp.bfloat16)


def strip(sources, targets, block):
    for at in range(0, targets.shape[1], LEAF):
        block[:, at : at + LEAF] = lax.rsqrt(dot(sources, targets[:, at : at + LEAF])).astype(jnp.bfloat16)


def listing(near, first):
    def listed(target, h):
        hit = near[0, target] == first + h
        for slot in range(1, near.shape[0]):
            hit = jnp.logical_or(hit, near[slot, target] == first + h)
        return hit.astype(jnp.float32)

    return listed


def near_kernel(near_list, own, total, charges, sources, targets, block, near, sem):
    copy = pltpu.make_async_copy(near_list, near, sem)
    copy.start()
    first = (lax.axis_index("leaf") * NSUB + lax.axis_index("sub")) * OWN
    listed = listing(near, first)
    charges[...] = own[:, 0:PTS].astype(jnp.bfloat16)
    for t in range(PTS // LANES):
        points = own[:, PTS + t * LANES : PTS + (t + 1) * LANES]
        sources[t * LANES : (t + 1) * LANES, :] = features(points, True).T
        targets[:, t * LANES : (t + 1) * LANES] = features(points, False)
    copy.wait()

    sums = [0.0] * OWN
    for step in range(OWN + 1):
        for d in range(REACH + 1):
            h = step
            if h + d < OWN:
                strip(
                    sources[h * LEAF : (h + 1) * LEAF, :],
                    targets[:, (h + d) * LEAF : (h + d + 1) * LEAF],
                    block.at[h % BUFFERS, d],
                )
            h = step - 1
            if h >= 0 and h + d < OWN:
                here = slice(h * LEAF, (h + 1) * LEAF)
                there = slice((h + d) * LEAF, (h + d + 1) * LEAF)
                values = block[h % BUFFERS, d]
                sums[h + d] += dot(charges[:, here], values) * listed(h + d, h)
                if d > 0:
                    sums[h] += dot(charges[:, there], values, NT) * listed(h, h + d)
        if step > 0:
            total[:, (step - 1) * LEAF : step * LEAF] = sums[step - 1]


def product_kernel(
    near_list, far_leaf, transfer, basis, own, from_left, from_right, total, table, beyond,
    out,
    down, coeffs, sources, targets, block, high, low, far_rows, near, far_cluster, sems,
):
    copies = [
        pltpu.make_async_copy(a, b, sems.at[i])
        for i, (a, b) in enumerate(((near_list, near), (own.at[:, AT_LIST:], far_cluster)))
    ]
    for copy in copies:
        copy.start()
    group = lax.axis_index("leaf")
    cluster = group * NSUB + lax.axis_index("sub")
    first = cluster * OWN

    out[...] = total[...]
    down[...] = jnp.zeros_like(down)
    at = 2 * NEAR_W
    pieces = []
    for start, width in ((AT_COEFFS, FAR_W), (AT_PROXY, FAR_W)):
        pieces.append((from_left[:, at : at + width], own[:, start : start + RANKS], from_right[:, at : at + width]))
        at += width
    coeffs[...] = jnp.concatenate(pieces[0], axis=1)
    for t, proxies in enumerate(pieces[1]):
        at = (0, FAR_W, FAR_W + RANKS)[t]
        sources[at : at + proxies.shape[1], :] = features(proxies, True).T
        targets[:, at : at + proxies.shape[1]] = features(proxies, False)
    for copy in copies:
        copy.wait()
    listed = listing(near, first)

    def edges(side, message):
        at = 0 if side == 0 else PTS - NEAR_W
        columns = features(message[:, NEAR_W : 2 * NEAR_W], True).T
        rows = features(own[:, PTS + at : PTS + at + NEAR_W], False)
        steps = []
        for i in range(REACH):
            h = i - REACH if side == 0 else OWN + i
            leaves = [g for g in range(OWN) if abs(g - h) <= REACH]
            skip, width = leaves[0] * LEAF - at, len(leaves) * LEAF
            values = block.at[REACH * side + i]

            def evaluate(i=i, values=values, skip=skip, width=width):
                strip(columns[i * LEAF : (i + 1) * LEAF], rows[:, skip : skip + width], values)

            def multiply(i=i, values=values, width=width):
                return dot(message[:, i * LEAF : (i + 1) * LEAF].astype(jnp.bfloat16), values[:, 0:width])

            def add(forward, h=h, leaves=leaves):
                for k, g in enumerate(leaves):
                    out[:, g * LEAF : (g + 1) * LEAF] += forward[:, k * LEAF : (k + 1) * LEAF] * listed(g, h)

            steps.append((evaluate, multiply, add))
        return steps

    span = 3 * LANES
    first_lanes = lax.broadcasted_iota(jnp.int32, (NRHS, LANES), 1) < RANK
    lists = jnp.where(far_leaf[...] >= 0, far_leaf[...] - first + FREACH, -1)
    far_rows[...] = jnp.full_like(far_rows, -1)
    for m in range(OWN // 2):
        at = FAR_W + m * LANES
        far_rows[:, at : at + LANES] = jnp.where(
            first_lanes,
            jnp.broadcast_to(lists[:, 2 * m : 2 * m + 1], (8, LANES)),
            jnp.broadcast_to(lists[:, 2 * m + 1 : 2 * m + 2], (8, LANES)),
        )
    lane_leaf = lax.broadcasted_iota(jnp.int32, (8, span), 1) // RANK

    def coupling(m):
        at = m * LANES
        to = at + LANES
        slot = m % BUFFERS

        def evaluate():
            values = lax.rsqrt(dot(sources[at : at + LANES, :], targets[:, to : to + span]))
            high[slot], low[slot] = split(values)

        def multiply():
            pair = coeffs[:, at : at + LANES]
            s_high, s_low = split(
                jnp.concatenate([jnp.where(first_lanes, pair, 0.0), jnp.where(first_lanes, 0.0, pair)], axis=0)
            )
            got = [dot(jnp.concatenate([s_high, s_low], axis=0), high[slot]), dot(s_high, low[slot])]
            if 2 * m >= FREACH:
                masked = []
                for i in range(2):
                    column = lists[:, 2 * m + i - FREACH : 2 * m + i - FREACH + 1]
                    hit = (lane_leaf + (2 * m + 2) == column).astype(jnp.float32)
                    masked.append(coeffs[:, to : to + span] * jnp.max(hit, axis=0, keepdims=True))
                t_high, t_low = split(jnp.concatenate(masked, axis=0))
                got.append(dot(jnp.concatenate([t_high, t_low], axis=0), high[slot], NT))
                got.append(dot(t_high, low[slot], NT))
            return got

        def add(got):
            forward = got[0][:16] + got[0][16:] + got[1]
            for i in range(2):
                hit = (far_rows[:, to : to + span] == 2 * m + i).astype(jnp.float32)
                hit = jnp.max(hit, axis=0, keepdims=True)
                down[:, to : to + span] += forward[8 * i : 8 * i + 8] * hit
            if len(got) > 2:
                reverse = got[2][:16] + got[2][16:] + got[3]
                down[:, at : at + LANES] += jnp.where(first_lanes, reverse[:8], reverse[8:])

        return evaluate, multiply, add

    steps = [coupling(m) for m in range((FREACH + OWN) // 2)]
    steps += edges(0, from_left) + edges(1, from_right)
    products = {}
    for i in range(len(steps) + AHEAD + 1):
        if i < len(steps):
            steps[i][0]()
        if 0 <= i - AHEAD < len(steps):
            products[i - AHEAD] = steps[i - AHEAD][1]()
        if 0 <= i - AHEAD - 1:
            steps[i - AHEAD - 1][2](products.pop(i - AHEAD - 1))

    plane = group // PLANE
    entries, kept = [], []
    for slot in range(FAR1):
        f = far_cluster[0, slot].astype(jnp.int32)
        valid = f >= 0
        f = jnp.where(valid, f, cluster)
        mine = f // (PLANE * NSUB) == plane
        place = lax.rem(f, PLANE * NSUB)
        e = jnp.where(mine, table[place], beyond[place])
        entries.append(e)
        kept.append(e * valid.astype(jnp.float32))
    parents, sources = [], []
    for m in range(len(entries) // 2):
        a, b = 2 * m, 2 * m + 1
        parents.append(jnp.where(first_lanes, kept[a], pltpu.roll(kept[b], RANK, 1)))
        sources.append(jnp.where(first_lanes, pltpu.roll(entries[a], RANK, 1), entries[b]))
    parents = jnp.concatenate(parents, axis=1)
    sources = jnp.concatenate(sources, axis=1)
    mine = table[lax.rem(cluster, PLANE * NSUB)].T[RANK : 2 * RANK]
    values = block_values(
        [mine[:, c : c + 1] for c in range(3)], [sources[c : c + 1, :] for c in range(3)]
    )
    coupled = dot3(parents, values, NT)

    pairs = range(OWN // 2)
    lowered = [dot3(coupled, jnp.reshape(transfer[2 * m : 2 * m + 2], (2 * RANK, RANK)), NT) for m in pairs]
    parts = []
    for m in pairs:
        pair = lowered[m] + down[:, FAR_W + m * LANES : FAR_W + (m + 1) * LANES]
        parts.append(
            split(jnp.concatenate([jnp.where(first_lanes, pair, 0.0), jnp.where(first_lanes, 0.0, pair)], axis=0))
        )
    far = [
        dot(jnp.concatenate(parts[m], axis=0), jnp.reshape(basis[2 * m : 2 * m + 2], (2 * RANK, LEAF)))
        for m in pairs
    ]
    for m in pairs:
        value = far[m][:16] + far[m][16:]
        for i in range(2):
            at = (2 * m + i) * LEAF
            out[:, at : at + LEAF] += value[8 * i : 8 * i + 8]


def shards(
    points, charges, order, basis, transfer, leaf_proxy, cluster_proxy, near, far_leaf, far_cluster
):
    vmem = pl.BlockSpec(memory_space=pltpu.VMEM)
    smem = pl.BlockSpec(memory_space=pltpu.SMEM)
    hbm = pl.BlockSpec(memory_space=pltpu.HBM)
    params = pltpu.CompilerParams(vmem_limit_bytes=48 * 2**20)
    f32 = jnp.float32
    leaf_proxy = leaf_proxy.transpose(1, 0, 2)
    cluster_proxy = cluster_proxy.transpose(1, 0, 2)
    near, far_leaf = near.transpose(1, 0), far_leaf.transpose(1, 0)
    given = (charges, points, order.reshape(PTS // LANES, LANES), basis, transfer, leaf_proxy, cluster_proxy, far_cluster)
    size = PLANE * NSUB
    own, right, left, spread = pl.pallas_call(
        prepare_kernel,
        in_specs=[hbm] * 8,
        out_specs=[vmem] * 4,
        out_shape=[
            jax.ShapeDtypeStruct((8, OWN_W), f32),
            jax.ShapeDtypeStruct((8, MSG), f32),
            jax.ShapeDtypeStruct((8, MSG), f32),
            jax.ShapeDtypeStruct((size, NRHS, LANES), f32),
        ],
        scratch_shapes=[pltpu.VMEM((2 * NRHS, PTS), jnp.bfloat16), pltpu.VMEM((NRHS, LANES), f32)]
        + [pltpu.VMEM(a.shape, a.dtype) for a in given]
        + [pltpu.SemaphoreType.DMA((8,))],
        name="prepare",
    )(*given)

    axes = ("leaf", "sub")
    groups, count = lax.axis_size("leaf"), lax.axis_size(axes)
    table = lax.all_to_all(
        spread, axes, 0, 0, tiled=True,
        axis_index_groups=[list(range(i, i + size)) for i in range(0, count, size)],
    )
    from_left = lax.ppermute(right, axes, [(i, i + 1) for i in range(count - 1)])
    from_right = lax.ppermute(left, axes, [(i + 1, i) for i in range(count - 1)])
    shift = [(g - PLANE, g) for g in range(PLANE, groups) if g % PLANE < HALF]
    shift += [(g + PLANE, g) for g in range(groups - PLANE) if g % PLANE >= HALF]
    beyond = lax.ppermute(table, "leaf", shift)
    total = pl.pallas_call(
        near_kernel,
        in_specs=[hbm, vmem],
        out_specs=vmem,
        out_shape=jax.ShapeDtypeStruct((NRHS, PTS), f32),
        scratch_shapes=[
            pltpu.VMEM((8, PTS), jnp.bfloat16),
            pltpu.VMEM((PTS, 64), jnp.bfloat16),
            pltpu.VMEM((64, PTS), jnp.bfloat16),
            pltpu.VMEM((BUFFERS, REACH + 1, LEAF, LEAF), jnp.bfloat16),
            pltpu.SMEM(near.shape, near.dtype),
            pltpu.SemaphoreType.DMA,
        ],
        cost_estimate=pl.CostEstimate(flops=9 * 10**9, bytes_accessed=10**6, transcendentals=3 * 10**6),
        compiler_params=params,
        name="near_field",
    )(near, own)
    far_window = OWN + 2 * FREACH
    return pl.pallas_call(
        product_kernel,
        in_specs=[hbm] + [vmem] * 9,
        out_specs=vmem,
        out_shape=jax.ShapeDtypeStruct((NRHS, PTS), f32),
        scratch_shapes=[
            pltpu.VMEM((NRHS, far_window * RANK), f32),
            pltpu.VMEM((8, far_window * RANK), f32),
            pltpu.VMEM((far_window * RANK, 64), jnp.bfloat16),
            pltpu.VMEM((64, far_window * RANK), jnp.bfloat16),
            pltpu.VMEM((2 * REACH, LEAF, REACH * LEAF), jnp.bfloat16),
            pltpu.VMEM((BUFFERS, 2 * RANK, 3 * LANES), jnp.bfloat16),
            pltpu.VMEM((BUFFERS, 2 * RANK, 3 * LANES), jnp.bfloat16),
            pltpu.VMEM((8, far_window * RANK), jnp.int32),
            pltpu.SMEM(near.shape, near.dtype),
            pltpu.SMEM((8, LANES), f32),
            pltpu.SemaphoreType.DMA((2,)),
        ],
        compiler_params=params,
        name="product",
    )(near, far_leaf, transfer, basis, own, from_left, from_right, total, table, beyond)


def solution(mesh):
    in_specs = (
        P(None, ("leaf", "sub")),
        P(None, ("leaf", "sub")),
        P(("leaf", "sub")),
        P(("leaf", "sub"), None, None),
        P(("leaf", "sub"), None, None),
        P(("leaf", "sub"), None, None),
        P(("leaf", "sub"), None, None),
        P(("leaf", "sub"), None),
        P(("leaf", "sub"), None),
        P(("leaf", "sub"), None),
    )
    out_specs = P(None, ("leaf", "sub"))
    return jax.shard_map(shards, mesh=mesh, in_specs=in_specs, out_specs=out_specs, check_vma=False)
```

```python
import jax
import jax.numpy as jnp
from jax import lax
from jax.experimental import pallas as pl
from jax.experimental.pallas import tpu as pltpu
from jax.sharding import PartitionSpec as P

LEAF = 256
RANK = 64
NRHS = 8
OWN = 16
REACH = 2
FREACH = 6
PLANE = 8
HALF = PLANE // 2
NSUB = 4
FAR1 = 16
PTS = OWN * LEAF
RANKS = OWN * RANK
LANES = 128
BUFFERS = 4
AHEAD = 2
SCALE = 16.0
SHIFT = 2.56

NEAR_W = REACH * LEAF
FAR_W = FREACH * RANK
MSG = 2 * NEAR_W + 2 * FAR_W
AT_CHARGES, AT_POINTS, AT_COEFFS, AT_PROXY = 0, PTS, 2 * PTS, 2 * PTS + RANKS
AT_LIST = 2 * PTS + 2 * RANKS
OWN_W = AT_LIST + LANES

NT = (((1,), (1,)), ((), ()))
NN = (((1,), (0,)), ((), ()))


def dot(a, b, dims=NN):
    return lax.dot_general(a, b, dims, preferred_element_type=jnp.float32)


def split(x):
    high = x.astype(jnp.bfloat16)
    return high, (x - high.astype(jnp.float32)).astype(jnp.bfloat16)


def dot3(a, b, dims=NN):
    rows = a.shape[0]
    a_high, a_low = split(a)
    b_high, b_low = split(b)
    both = dot(jnp.concatenate([a_high, a_low], axis=0), b_high, dims)
    return both[:rows] + both[rows:] + dot(a_high, b_low, dims)


ALONG_LANES = lax.GatherDimensionNumbers(
    offset_dims=(), collapsed_slice_dims=(1,), start_index_map=(1,), operand_batching_dims=(0,),
    start_indices_batching_dims=(0,),
)


def picked(source, index, count, dtype):
    low = jnp.bitwise_and(index, dtype(LANES - 1))[..., None]
    bits, k = [], 1
    while k < count:
        bits.append(jnp.bitwise_and(index, dtype(k * LANES)) != 0)
        k *= 2

    def among(first, level):
        if level == 0:
            return lax.gather(
                source(first), low, ALONG_LANES, (1, 1), mode=lax.GatherScatterMode.PROMISE_IN_BOUNDS
            )
        size = 1 << (level - 1)
        return jnp.where(bits[level - 1], among(first + size, level - 1), among(first, level - 1))

    return among(0, len(bits))


def prepare_kernel(
    charges, points, order, basis, transfer, leaf_proxy, cluster_proxy, far_cluster,
    own, inner, outer, spread,
    twice, entry, charges_in, points_in, order_in, basis_in, transfer_in, leaf_proxy_in, cluster_proxy_in, far_cluster_in, sems,
):
    copies = [
        pltpu.make_async_copy(a, b, sems.at[i])
        for i, (a, b) in enumerate(
            (
                (order, order_in), (charges, charges_in), (points, points_in), (leaf_proxy, leaf_proxy_in),
                (cluster_proxy, cluster_proxy_in), (far_cluster, far_cluster_in), (basis, basis_in),
                (transfer, transfer_in),
            )
        )
    ]
    for copy in copies:
        copy.start()
    own[:, AT_PROXY : AT_PROXY + RANKS] = jnp.zeros((8, RANKS), jnp.float32)
    entry[...] = jnp.zeros((NRHS, LANES), jnp.float32)
    own[:, AT_POINTS : AT_POINTS + PTS] = jnp.zeros((8, PTS), jnp.float32)
    for copy in copies[:3]:
        copy.wait()
    blocks = PTS // LANES
    both = charges_in[...].astype(jnp.float32)
    twice[...] = jnp.concatenate([both, both], axis=0).astype(jnp.bfloat16)

    for i in range(blocks // 2):
        index = jnp.concatenate(
            [jnp.broadcast_to(order_in[2 * i + k : 2 * i + k + 1, :], (NRHS, LANES)) for k in range(2)], axis=0
        ).astype(jnp.int16)
        got = picked(
            lambda k: twice[:, k * LANES : (k + 1) * LANES], index, blocks, jnp.int16
        ).astype(jnp.float32)
        for k in range(2):
            own[:, (2 * i + k) * LANES : (2 * i + k + 1) * LANES] = got[NRHS * k : NRHS * (k + 1)]

    for j in range(blocks // 8):
        index = order_in[8 * j : 8 * j + 8, :]
        for c in range(3):
            got = picked(
                lambda k: jnp.broadcast_to(points_in[c : c + 1, k * LANES : (k + 1) * LANES], (8, LANES)),
                index, blocks, jnp.int32,
            ) * SCALE
            for s in range(8):
                at = AT_POINTS + (8 * j + s) * LANES
                own[c : c + 1, at : at + LANES] = got[s : s + 1]

    for copy in copies[3:]:
        copy.wait()
    for g in range(OWN):
        at = AT_PROXY + g * RANK
        own[0:3, at : at + RANK] = leaf_proxy_in[:, g, :] * SCALE

    own[:, AT_LIST:] = jnp.zeros((8, LANES), jnp.float32)
    own[0:1, AT_LIST : AT_LIST + far_cluster_in.shape[1]] = far_cluster_in[...].astype(jnp.float32)

    first_half = lax.broadcasted_iota(jnp.int32, (NRHS, LANES), 1) < RANK
    parent = jnp.zeros((NRHS, RANK), jnp.float32)
    pairs = range(OWN // 2)
    both = [
        dot(
            jnp.concatenate(
                [own[:, g * LEAF : (g + 1) * LEAF].astype(jnp.bfloat16) for g in (2 * m, 2 * m + 1)], axis=0
            ),
            jnp.reshape(basis_in[2 * m : 2 * m + 2], (2 * RANK, LEAF)),
            NT,
        )
        for m in pairs
    ]
    coeffs = [jnp.where(first_half, both[m][:NRHS], both[m][NRHS:]) for m in pairs]
    for m in pairs:
        own[:, AT_COEFFS + m * LANES : AT_COEFFS + (m + 1) * LANES] = coeffs[m]
        parent += dot3(coeffs[m], jnp.reshape(transfer_in[2 * m : 2 * m + 2], (2 * RANK, RANK)))

    entry[:, 0:RANK] = parent
    entry[0:3, RANK : 2 * RANK] = cluster_proxy_in[:, 0, :] * SCALE

    for place in range(PLANE * NSUB):
        spread[place] = entry[...]

    odd = lax.rem(lax.axis_index("sub"), 2) == 1
    at = 0
    for start, whole, width in (
        (AT_CHARGES, PTS, NEAR_W), (AT_POINTS, PTS, NEAR_W),
        (AT_COEFFS, RANKS, FAR_W), (AT_PROXY, RANKS, FAR_W),
    ):
        low = own[:, start : start + width]
        high = own[:, start + whole - width : start + whole]
        inner[:, at : at + width] = jnp.where(odd, low, high)
        outer[:, at : at + width] = jnp.where(odd, high, low)
        at += width


def block_values(columns, rows):
    d0 = columns[0] - rows[0]
    d1 = columns[1] - rows[1]
    d2 = columns[2] - rows[2]
    return lax.rsqrt(d0 * d0 + d1 * d1 + d2 * d2 + SHIFT)


def features(points, as_source):
    row = lax.broadcasted_iota(jnp.int32, points.shape, 0)
    h = jnp.floor(points * 2.0 + 0.5) * 0.5
    l = points - h
    l1 = l.astype(jnp.bfloat16).astype(jnp.float32)
    l2 = l - l1
    n = jnp.sum(h * h, axis=0, keepdims=True)
    n1 = jnp.floor(n * (1 / 128) + 0.5) * 128.0
    n2 = n - n1
    s = jnp.sum((2.0 * h + l) * l, axis=0, keepdims=True) + SHIFT / 2
    s1 = s.astype(jnp.bfloat16).astype(jnp.float32)
    s2 = (s - s1).astype(jnp.bfloat16).astype(jnp.float32)
    s3 = s - s1 - s2

    def stack(vector, *others):
        for i, other in enumerate(others):
            vector = jnp.where(row == 3 + i, other, vector)
        return vector

    if as_source:
        groups = [
            stack(h, n1, n2, 1.0, 1.0), stack(h, s1, s2, s3, 1.0, 1.0), stack(h, 1.0), l1, l2, l1, l1, l2
        ]
    else:
        h, l1, l2 = -2.0 * h, -2.0 * l1, -2.0 * l2
        groups = [
            stack(h, 1.0, 1.0, n1, n2), stack(l1, 1.0, 1.0, 1.0, s1, s2), stack(l2, s3), h, h, l1, l2, l1
        ]
    return jnp.concatenate(groups, axis=0).astype(jnp.bfloat16)


def strip(sources, targets, block):
    for at in range(0, targets.shape[1], LEAF):
        block[:, at : at + LEAF] = lax.rsqrt(dot(sources, targets[:, at : at + LEAF])).astype(jnp.bfloat16)


def listing(near, first):
    def listed(target, h):
        hit = near[0, target] == first + h
        for slot in range(1, near.shape[0]):
            hit = jnp.logical_or(hit, near[slot, target] == first + h)
        return hit.astype(jnp.float32)

    return listed


def near_kernel(near_list, own, total, charges, sources, targets, block, near, sem):
    copy = pltpu.make_async_copy(near_list, near, sem)
    copy.start()
    first = (lax.axis_index("leaf") * NSUB + lax.axis_index("sub")) * OWN
    listed = listing(near, first)
    charges[...] = own[:, 0:PTS].astype(jnp.bfloat16)
    for t in range(PTS // LANES):
        points = own[:, PTS + t * LANES : PTS + (t + 1) * LANES]
        sources[t * LANES : (t + 1) * LANES, :] = features(points, True).T
        targets[:, t * LANES : (t + 1) * LANES] = features(points, False)
    copy.wait()

    sums = [0.0] * OWN
    for step in range(OWN + 1):
        for d in range(REACH + 1):
            h = step
            if h + d < OWN:
                strip(
                    sources[h * LEAF : (h + 1) * LEAF, :],
                    targets[:, (h + d) * LEAF : (h + d + 1) * LEAF],
                    block.at[h % BUFFERS, d],
                )
            h = step - 1
            if h >= 0 and h + d < OWN:
                here = slice(h * LEAF, (h + 1) * LEAF)
                there = slice((h + d) * LEAF, (h + d + 1) * LEAF)
                values = block[h % BUFFERS, d]
                sums[h + d] += dot(charges[:, here], values) * listed(h + d, h)
                if d > 0:
                    sums[h] += dot(charges[:, there], values, NT) * listed(h, h + d)
        if step > 0:
            total[:, (step - 1) * LEAF : step * LEAF] = sums[step - 1]


def product_kernel(
    near_list, far_leaf, transfer, basis, own, outer, inner, total, table, beyond,
    out,
    down, coeffs, sources, targets, block, high, low, far_rows, near, far_cluster, sems,
):
    copies = [
        pltpu.make_async_copy(a, b, sems.at[i])
        for i, (a, b) in enumerate(((near_list, near), (own.at[:, AT_LIST:], far_cluster)))
    ]
    for copy in copies:
        copy.start()
    group = lax.axis_index("leaf")
    cluster = group * NSUB + lax.axis_index("sub")
    first = cluster * OWN
    odd = lax.rem(lax.axis_index("sub"), 2) == 1
    from_left = jnp.where(odd, inner[...], outer[...])
    from_right = jnp.where(odd, outer[...], inner[...])

    out[...] = total[...]
    down[...] = jnp.zeros_like(down)
    at = 2 * NEAR_W
    pieces = []
    for start, width in ((AT_COEFFS, FAR_W), (AT_PROXY, FAR_W)):
        pieces.append((from_left[:, at : at + width], own[:, start : start + RANKS], from_right[:, at : at + width]))
        at += width
    coeffs[...] = jnp.concatenate(pieces[0], axis=1)
    for t, proxies in enumerate(pieces[1]):
        at = (0, FAR_W, FAR_W + RANKS)[t]
        sources[at : at + proxies.shape[1], :] = features(proxies, True).T
        targets[:, at : at + proxies.shape[1]] = features(proxies, False)
    for copy in copies:
        copy.wait()
    listed = listing(near, first)

    def edges(side, message):
        at = 0 if side == 0 else PTS - NEAR_W
        columns = features(message[:, NEAR_W : 2 * NEAR_W], True).T
        rows = features(own[:, PTS + at : PTS + at + NEAR_W], False)
        steps = []
        for i in range(REACH):
            h = i - REACH if side == 0 else OWN + i
            leaves = [g for g in range(OWN) if abs(g - h) <= REACH]
            skip, width = leaves[0] * LEAF - at, len(leaves) * LEAF
            values = block.at[REACH * side + i]

            def evaluate(i=i, values=values, skip=skip, width=width):
                strip(columns[i * LEAF : (i + 1) * LEAF], rows[:, skip : skip + width], values)

            def multiply(i=i, values=values, width=width):
                return dot(message[:, i * LEAF : (i + 1) * LEAF].astype(jnp.bfloat16), values[:, 0:width])

            def add(forward, h=h, leaves=leaves):
                for k, g in enumerate(leaves):
                    out[:, g * LEAF : (g + 1) * LEAF] += forward[:, k * LEAF : (k + 1) * LEAF] * listed(g, h)

            steps.append((evaluate, multiply, add))
        return steps

    span = 3 * LANES
    first_lanes = lax.broadcasted_iota(jnp.int32, (NRHS, LANES), 1) < RANK
    lists = jnp.where(far_leaf[...] >= 0, far_leaf[...] - first + FREACH, -1)
    far_rows[...] = jnp.full_like(far_rows, -1)
    for m in range(OWN // 2):
        at = FAR_W + m * LANES
        far_rows[:, at : at + LANES] = jnp.where(
            first_lanes,
            jnp.broadcast_to(lists[:, 2 * m : 2 * m + 1], (8, LANES)),
            jnp.broadcast_to(lists[:, 2 * m + 1 : 2 * m + 2], (8, LANES)),
        )
    lane_leaf = lax.broadcasted_iota(jnp.int32, (8, span), 1) // RANK

    def coupling(m):
        at = m * LANES
        to = at + LANES
        slot = m % BUFFERS

        def evaluate():
            values = lax.rsqrt(dot(sources[at : at + LANES, :], targets[:, to : to + span]))
            high[slot], low[slot] = split(values)

        def multiply():
            pair = coeffs[:, at : at + LANES]
            s_high, s_low = split(
                jnp.concatenate([jnp.where(first_lanes, pair, 0.0), jnp.where(first_lanes, 0.0, pair)], axis=0)
            )
            got = [dot(jnp.concatenate([s_high, s_low], axis=0), high[slot]), dot(s_high, low[slot])]
            if 2 * m >= FREACH:
                masked = []
                for i in range(2):
                    column = lists[:, 2 * m + i - FREACH : 2 * m + i - FREACH + 1]
                    hit = (lane_leaf + (2 * m + 2) == column).astype(jnp.float32)
                    masked.append(coeffs[:, to : to + span] * jnp.max(hit, axis=0, keepdims=True))
                t_high, t_low = split(jnp.concatenate(masked, axis=0))
                got.append(dot(jnp.concatenate([t_high, t_low], axis=0), high[slot], NT))
                got.append(dot(t_high, low[slot], NT))
            return got

        def add(got):
            forward = got[0][:16] + got[0][16:] + got[1]
            for i in range(2):
                hit = (far_rows[:, to : to + span] == 2 * m + i).astype(jnp.float32)
                hit = jnp.max(hit, axis=0, keepdims=True)
                down[:, to : to + span] += forward[8 * i : 8 * i + 8] * hit
            if len(got) > 2:
                reverse = got[2][:16] + got[2][16:] + got[3]
                down[:, at : at + LANES] += jnp.where(first_lanes, reverse[:8], reverse[8:])

        return evaluate, multiply, add

    steps = [coupling(m) for m in range((FREACH + OWN) // 2)]
    steps += edges(0, from_left) + edges(1, from_right)
    products = {}
    for i in range(len(steps) + AHEAD + 1):
        if i < len(steps):
            steps[i][0]()
        if 0 <= i - AHEAD < len(steps):
            products[i - AHEAD] = steps[i - AHEAD][1]()
        if 0 <= i - AHEAD - 1:
            steps[i - AHEAD - 1][2](products.pop(i - AHEAD - 1))

    plane = group // PLANE
    entries, kept = [], []
    for slot in range(FAR1):
        f = far_cluster[0, slot].astype(jnp.int32)
        valid = f >= 0
        f = jnp.where(valid, f, cluster)
        mine = f // (PLANE * NSUB) == plane
        place = lax.rem(f, PLANE * NSUB)
        e = jnp.where(mine, table[place], beyond[place])
        entries.append(e)
        kept.append(e * valid.astype(jnp.float32))
    parents, sources = [], []
    for m in range(len(entries) // 2):
        a, b = 2 * m, 2 * m + 1
        parents.append(jnp.where(first_lanes, kept[a], pltpu.roll(kept[b], RANK, 1)))
        sources.append(jnp.where(first_lanes, pltpu.roll(entries[a], RANK, 1), entries[b]))
    parents = jnp.concatenate(parents, axis=1)
    sources = jnp.concatenate(sources, axis=1)
    mine = table[lax.rem(cluster, PLANE * NSUB)].T[RANK : 2 * RANK]
    values = block_values(
        [mine[:, c : c + 1] for c in range(3)], [sources[c : c + 1, :] for c in range(3)]
    )
    coupled = dot3(parents, values, NT)

    pairs = range(OWN // 2)
    lowered = [dot3(coupled, jnp.reshape(transfer[2 * m : 2 * m + 2], (2 * RANK, RANK)), NT) for m in pairs]
    parts = []
    for m in pairs:
        pair = lowered[m] + down[:, FAR_W + m * LANES : FAR_W + (m + 1) * LANES]
        parts.append(
            split(jnp.concatenate([jnp.where(first_lanes, pair, 0.0), jnp.where(first_lanes, 0.0, pair)], axis=0))
        )
    far = [
        dot(jnp.concatenate(parts[m], axis=0), jnp.reshape(basis[2 * m : 2 * m + 2], (2 * RANK, LEAF)))
        for m in pairs
    ]
    for m in pairs:
        value = far[m][:16] + far[m][16:]
        for i in range(2):
            at = (2 * m + i) * LEAF
            out[:, at : at + LEAF] += value[8 * i : 8 * i + 8]


def shards(
    points, charges, order, basis, transfer, leaf_proxy, cluster_proxy, near, far_leaf, far_cluster
):
    vmem = pl.BlockSpec(memory_space=pltpu.VMEM)
    smem = pl.BlockSpec(memory_space=pltpu.SMEM)
    hbm = pl.BlockSpec(memory_space=pltpu.HBM)
    params = pltpu.CompilerParams(vmem_limit_bytes=48 * 2**20)
    f32 = jnp.float32
    leaf_proxy = leaf_proxy.transpose(1, 0, 2)
    cluster_proxy = cluster_proxy.transpose(1, 0, 2)
    near, far_leaf = near.transpose(1, 0), far_leaf.transpose(1, 0)
    given = (charges, points, order.reshape(PTS // LANES, LANES), basis, transfer, leaf_proxy, cluster_proxy, far_cluster)
    size = PLANE * NSUB
    own, inner, outer, spread = pl.pallas_call(
        prepare_kernel,
        in_specs=[hbm] * 8,
        out_specs=[vmem] * 4,
        out_shape=[
            jax.ShapeDtypeStruct((8, OWN_W), f32),
            jax.ShapeDtypeStruct((8, MSG), f32),
            jax.ShapeDtypeStruct((8, MSG), f32),
            jax.ShapeDtypeStruct((size, NRHS, LANES), f32),
        ],
        scratch_shapes=[pltpu.VMEM((2 * NRHS, PTS), jnp.bfloat16), pltpu.VMEM((NRHS, LANES), f32)]
        + [pltpu.VMEM(a.shape, a.dtype) for a in given]
        + [pltpu.SemaphoreType.DMA((8,))],
        name="prepare",
    )(*given)

    axes = ("leaf", "sub")
    groups, count = lax.axis_size("leaf"), lax.axis_size(axes)
    table = lax.all_to_all(
        spread, axes, 0, 0, tiled=True,
        axis_index_groups=[list(range(i, i + size)) for i in range(0, count, size)],
    )
    outer = lax.ppermute(outer, axes, [(i, ((i + 1) ^ 1) - 1) for i in range(1, count - 1)])
    inner = lax.ppermute(inner, axes, [(i, i ^ 1) for i in range(count)])
    shift = [(g - PLANE, g) for g in range(PLANE, groups) if g % PLANE < HALF]
    shift += [(g + PLANE, g) for g in range(groups - PLANE) if g % PLANE >= HALF]
    beyond = lax.ppermute(table, "leaf", shift)
    total = pl.pallas_call(
        near_kernel,
        in_specs=[hbm, vmem],
        out_specs=vmem,
        out_shape=jax.ShapeDtypeStruct((NRHS, PTS), f32),
        scratch_shapes=[
            pltpu.VMEM((8, PTS), jnp.bfloat16),
            pltpu.VMEM((PTS, 64), jnp.bfloat16),
            pltpu.VMEM((64, PTS), jnp.bfloat16),
            pltpu.VMEM((BUFFERS, REACH + 1, LEAF, LEAF), jnp.bfloat16),
            pltpu.SMEM(near.shape, near.dtype),
            pltpu.SemaphoreType.DMA,
        ],
        cost_estimate=pl.CostEstimate(flops=9 * 10**9, bytes_accessed=10**6, transcendentals=3 * 10**6),
        compiler_params=params,
        name="near_field",
    )(near, own)
    far_window = OWN + 2 * FREACH
    return pl.pallas_call(
        product_kernel,
        in_specs=[hbm] + [vmem] * 9,
        out_specs=vmem,
        out_shape=jax.ShapeDtypeStruct((NRHS, PTS), f32),
        scratch_shapes=[
            pltpu.VMEM((NRHS, far_window * RANK), f32),
            pltpu.VMEM((8, far_window * RANK), f32),
            pltpu.VMEM((far_window * RANK, 64), jnp.bfloat16),
            pltpu.VMEM((64, far_window * RANK), jnp.bfloat16),
            pltpu.VMEM((2 * REACH, LEAF, REACH * LEAF), jnp.bfloat16),
            pltpu.VMEM((BUFFERS, 2 * RANK, 3 * LANES), jnp.bfloat16),
            pltpu.VMEM((BUFFERS, 2 * RANK, 3 * LANES), jnp.bfloat16),
            pltpu.VMEM((8, far_window * RANK), jnp.int32),
            pltpu.SMEM(near.shape, near.dtype),
            pltpu.SMEM((8, LANES), f32),
            pltpu.SemaphoreType.DMA((2,)),
        ],
        compiler_params=params,
        name="product",
    )(near, far_leaf, transfer, basis, own, outer, inner, total, table, beyond)


def solution(mesh):
    in_specs = (
        P(None, ("leaf", "sub")),
        P(None, ("leaf", "sub")),
        P(("leaf", "sub")),
        P(("leaf", "sub"), None, None),
        P(("leaf", "sub"), None, None),
        P(("leaf", "sub"), None, None),
        P(("leaf", "sub"), None, None),
        P(("leaf", "sub"), None),
        P(("leaf", "sub"), None),
        P(("leaf", "sub"), None),
    )
    out_specs = P(None, ("leaf", "sub"))
    return jax.shard_map(shards, mesh=mesh, in_specs=in_specs, out_specs=out_specs, check_vma=False)
```

```python
import jax
import jax.numpy as jnp
from jax import lax
from jax.experimental import pallas as pl
from jax.experimental.pallas import tpu as pltpu
from jax.sharding import PartitionSpec as P

LEAF = 256
RANK = 64
NRHS = 8
OWN = 16
REACH = 2
FREACH = 6
PLANE = 8
HALF = PLANE // 2
NSUB = 4
FAR1 = 16
PTS = OWN * LEAF
RANKS = OWN * RANK
LANES = 128
BUFFERS = 6
LATER = 3
AHEAD = 3
SCALE = 16.0
SHIFT = 2.56

NEAR_W = REACH * LEAF
FAR_W = FREACH * RANK
MSG = 2 * NEAR_W + 2 * FAR_W
AT_CHARGES, AT_POINTS, AT_COEFFS, AT_PROXY = 0, PTS, 2 * PTS, 2 * PTS + RANKS
AT_LIST = 2 * PTS + 2 * RANKS
OWN_W = AT_LIST + LANES

NT = (((1,), (1,)), ((), ()))
NN = (((1,), (0,)), ((), ()))


def dot(a, b, dims=NN):
    return lax.dot_general(a, b, dims, preferred_element_type=jnp.float32)


def split(x):
    high = x.astype(jnp.bfloat16)
    return high, (x - high.astype(jnp.float32)).astype(jnp.bfloat16)


def dot3(a, b, dims=NN):
    rows = a.shape[0]
    a_high, a_low = split(a)
    b_high, b_low = split(b)
    both = dot(jnp.concatenate([a_high, a_low], axis=0), b_high, dims)
    return both[:rows] + both[rows:] + dot(a_high, b_low, dims)


ALONG_LANES = lax.GatherDimensionNumbers(
    offset_dims=(), collapsed_slice_dims=(1,), start_index_map=(1,), operand_batching_dims=(0,),
    start_indices_batching_dims=(0,),
)


def picked(source, index, count, dtype):
    low = jnp.bitwise_and(index, dtype(LANES - 1))[..., None]
    bits, k = [], 1
    while k < count:
        bits.append(jnp.bitwise_and(index, dtype(k * LANES)) != 0)
        k *= 2

    def among(first, level):
        if level == 0:
            return lax.gather(
                source(first), low, ALONG_LANES, (1, 1), mode=lax.GatherScatterMode.PROMISE_IN_BOUNDS
            )
        size = 1 << (level - 1)
        return jnp.where(bits[level - 1], among(first + size, level - 1), among(first, level - 1))

    return among(0, len(bits))


def prepare_kernel(
    charges, points, order, basis, transfer, leaf_proxy, cluster_proxy, far_cluster,
    own, inner, outer, spread,
    twice, entry, charges_in, points_in, order_in, basis_in, transfer_in, leaf_proxy_in, cluster_proxy_in, far_cluster_in, sems,
):
    copies = [
        pltpu.make_async_copy(a, b, sems.at[i])
        for i, (a, b) in enumerate(
            (
                (order, order_in), (charges, charges_in), (points, points_in), (leaf_proxy, leaf_proxy_in),
                (cluster_proxy, cluster_proxy_in), (far_cluster, far_cluster_in), (basis, basis_in),
                (transfer, transfer_in),
            )
        )
    ]
    for copy in copies:
        copy.start()
    own[:, AT_PROXY : AT_PROXY + RANKS] = jnp.zeros((8, RANKS), jnp.float32)
    entry[...] = jnp.zeros((NRHS, LANES), jnp.float32)
    own[:, AT_POINTS : AT_POINTS + PTS] = jnp.zeros((8, PTS), jnp.float32)
    for copy in copies[:3]:
        copy.wait()
    blocks = PTS // LANES
    both = charges_in[...].astype(jnp.float32)
    twice[...] = jnp.concatenate([both, both], axis=0).astype(jnp.bfloat16)

    for i in range(blocks // 2):
        index = jnp.concatenate(
            [jnp.broadcast_to(order_in[2 * i + k : 2 * i + k + 1, :], (NRHS, LANES)) for k in range(2)], axis=0
        ).astype(jnp.int16)
        got = picked(
            lambda k: twice[:, k * LANES : (k + 1) * LANES], index, blocks, jnp.int16
        ).astype(jnp.float32)
        for k in range(2):
            own[:, (2 * i + k) * LANES : (2 * i + k + 1) * LANES] = got[NRHS * k : NRHS * (k + 1)]

    for copy in copies[3:]:
        copy.wait()
    for g in range(OWN):
        at = AT_PROXY + g * RANK
        own[0:3, at : at + RANK] = leaf_proxy_in[:, g, :] * SCALE
    own[:, AT_LIST:] = jnp.zeros((8, LANES), jnp.float32)
    own[0:1, AT_LIST : AT_LIST + far_cluster_in.shape[1]] = far_cluster_in[...].astype(jnp.float32)

    first_half = lax.broadcasted_iota(jnp.int32, (NRHS, LANES), 1) < RANK
    parent = jnp.zeros((NRHS, RANK), jnp.float32)
    for j in range(blocks // 8):
        pairs = range(2 * j, 2 * j + 2)
        both = [
            dot(
                jnp.concatenate(
                    [own[:, g * LEAF : (g + 1) * LEAF].astype(jnp.bfloat16) for g in (2 * m, 2 * m + 1)], axis=0
                ),
                jnp.reshape(basis_in[2 * m : 2 * m + 2], (2 * RANK, LEAF)),
                NT,
            )
            for m in pairs
        ]
        index = order_in[8 * j : 8 * j + 8, :]
        for c in range(3):
            got = picked(
                lambda k: jnp.broadcast_to(points_in[c : c + 1, k * LANES : (k + 1) * LANES], (8, LANES)),
                index, blocks, jnp.int32,
            ) * SCALE
            for s in range(8):
                at = AT_POINTS + (8 * j + s) * LANES
                own[c : c + 1, at : at + LANES] = got[s : s + 1]
        for m, pair in zip(pairs, both):
            coeffs = jnp.where(first_half, pair[:NRHS], pair[NRHS:])
            own[:, AT_COEFFS + m * LANES : AT_COEFFS + (m + 1) * LANES] = coeffs
            parent += dot3(coeffs, jnp.reshape(transfer_in[2 * m : 2 * m + 2], (2 * RANK, RANK)))

    entry[:, 0:RANK] = parent
    entry[0:3, RANK : 2 * RANK] = cluster_proxy_in[:, 0, :] * SCALE

    for place in range(PLANE * NSUB):
        spread[place] = entry[...]

    odd = lax.rem(lax.axis_index("sub"), 2) == 1
    at = 0
    for start, whole, width in (
        (AT_CHARGES, PTS, NEAR_W), (AT_POINTS, PTS, NEAR_W),
        (AT_COEFFS, RANKS, FAR_W), (AT_PROXY, RANKS, FAR_W),
    ):
        low = own[:, start : start + width]
        high = own[:, start + whole - width : start + whole]
        inner[:, at : at + width] = jnp.where(odd, low, high)
        outer[:, at : at + width] = jnp.where(odd, high, low)
        at += width


def block_values(columns, rows):
    d0 = columns[0] - rows[0]
    d1 = columns[1] - rows[1]
    d2 = columns[2] - rows[2]
    return lax.rsqrt(d0 * d0 + d1 * d1 + d2 * d2 + SHIFT)


def features(points, as_source):
    row = lax.broadcasted_iota(jnp.int32, points.shape, 0)
    h = jnp.floor(points * 2.0 + 0.5) * 0.5
    l = points - h
    l1 = l.astype(jnp.bfloat16).astype(jnp.float32)
    l2 = l - l1
    n = jnp.sum(h * h, axis=0, keepdims=True)
    n1 = jnp.floor(n * (1 / 128) + 0.5) * 128.0
    n2 = n - n1
    s = jnp.sum((2.0 * h + l) * l, axis=0, keepdims=True) + SHIFT / 2
    s1 = s.astype(jnp.bfloat16).astype(jnp.float32)
    s2 = (s - s1).astype(jnp.bfloat16).astype(jnp.float32)
    s3 = s - s1 - s2

    def stack(vector, *others):
        for i, other in enumerate(others):
            vector = jnp.where(row == 3 + i, other, vector)
        return vector

    if as_source:
        groups = [
            stack(h, n1, n2, 1.0, 1.0), stack(h, s1, s2, s3, 1.0, 1.0), stack(h, 1.0), l1, l2, l1, l1, l2
        ]
    else:
        h, l1, l2 = -2.0 * h, -2.0 * l1, -2.0 * l2
        groups = [
            stack(h, 1.0, 1.0, n1, n2), stack(l1, 1.0, 1.0, 1.0, s1, s2), stack(l2, s3), h, h, l1, l2, l1
        ]
    return jnp.concatenate(groups, axis=0).astype(jnp.bfloat16)


def strip(sources, targets, block):
    for at in range(0, targets.shape[1], LEAF):
        block[:, at : at + LEAF] = lax.rsqrt(dot(sources, targets[:, at : at + LEAF])).astype(jnp.bfloat16)


def listing(near, first):
    def listed(target, h):
        hit = near[0, target] == first + h
        for slot in range(1, near.shape[0]):
            hit = jnp.logical_or(hit, near[slot, target] == first + h)
        return hit.astype(jnp.float32)

    return listed


def near_kernel(near_list, own, total, charges, sources, targets, block, near, sem):
    copy = pltpu.make_async_copy(near_list, near, sem)
    copy.start()
    first = (lax.axis_index("leaf") * NSUB + lax.axis_index("sub")) * OWN
    listed = listing(near, first)
    charges[...] = own[:, 0:PTS].astype(jnp.bfloat16)
    for t in range(PTS // LANES):
        points = own[:, PTS + t * LANES : PTS + (t + 1) * LANES]
        sources[t * LANES : (t + 1) * LANES, :] = features(points, True).T
        targets[:, t * LANES : (t + 1) * LANES] = features(points, False)
    copy.wait()

    sums = [0.0] * OWN
    for step in range(OWN + LATER):
        for d in range(REACH + 1):
            h = step
            if h + d < OWN:
                strip(
                    sources[h * LEAF : (h + 1) * LEAF, :],
                    targets[:, (h + d) * LEAF : (h + d + 1) * LEAF],
                    block.at[h % BUFFERS, d],
                )
            h = step - LATER
            if h >= 0 and h + d < OWN:
                here = slice(h * LEAF, (h + 1) * LEAF)
                there = slice((h + d) * LEAF, (h + d + 1) * LEAF)
                values = block[h % BUFFERS, d]
                sums[h + d] += dot(charges[:, here], values) * listed(h + d, h)
                if d > 0:
                    sums[h] += dot(charges[:, there], values, NT) * listed(h, h + d)
        if step >= LATER:
            total[:, (step - LATER) * LEAF : (step - LATER + 1) * LEAF] = sums[step - LATER]


def product_kernel(
    near_list, far_leaf, transfer, basis, own, outer, inner, total, table, beyond,
    out,
    down, coeffs, sources, targets, block, high, low, far_rows, near, far_cluster, sems,
):
    copies = [
        pltpu.make_async_copy(a, b, sems.at[i])
        for i, (a, b) in enumerate(((near_list, near), (own.at[:, AT_LIST:], far_cluster)))
    ]
    for copy in copies:
        copy.start()
    group = lax.axis_index("leaf")
    cluster = group * NSUB + lax.axis_index("sub")
    first = cluster * OWN
    odd = lax.rem(lax.axis_index("sub"), 2) == 1
    from_left = jnp.where(odd, inner[...], outer[...])
    from_right = jnp.where(odd, outer[...], inner[...])

    out[...] = total[...]
    down[...] = jnp.zeros_like(down)
    at = 2 * NEAR_W
    pieces = []
    for start, width in ((AT_COEFFS, FAR_W), (AT_PROXY, FAR_W)):
        pieces.append((from_left[:, at : at + width], own[:, start : start + RANKS], from_right[:, at : at + width]))
        at += width
    coeffs[...] = jnp.concatenate(pieces[0], axis=1)
    for t, proxies in enumerate(pieces[1]):
        at = (0, FAR_W, FAR_W + RANKS)[t]
        sources[at : at + proxies.shape[1], :] = features(proxies, True).T
        targets[:, at : at + proxies.shape[1]] = features(proxies, False)
    listed = listing(near, first)

    def edges(side, message):
        at = 0 if side == 0 else PTS - NEAR_W
        columns = features(message[:, NEAR_W : 2 * NEAR_W], True).T
        rows = features(own[:, PTS + at : PTS + at + NEAR_W], False)
        steps = []
        for i in range(REACH):
            h = i - REACH if side == 0 else OWN + i
            leaves = [g for g in range(OWN) if abs(g - h) <= REACH]
            skip, width = leaves[0] * LEAF - at, len(leaves) * LEAF
            values = block.at[REACH * side + i]

            def evaluate(i=i, values=values, skip=skip, width=width):
                strip(columns[i * LEAF : (i + 1) * LEAF], rows[:, skip : skip + width], values)

            def multiply(i=i, values=values, width=width):
                return dot(message[:, i * LEAF : (i + 1) * LEAF].astype(jnp.bfloat16), values[:, 0:width])

            def add(forward, h=h, leaves=leaves):
                for k, g in enumerate(leaves):
                    out[:, g * LEAF : (g + 1) * LEAF] += forward[:, k * LEAF : (k + 1) * LEAF] * listed(g, h)

            steps.append((evaluate, multiply, add))
        return steps

    span = 3 * LANES
    first_lanes = lax.broadcasted_iota(jnp.int32, (NRHS, LANES), 1) < RANK
    lists = jnp.where(far_leaf[...] >= 0, far_leaf[...] - first + FREACH, -1)
    far_rows[...] = jnp.full_like(far_rows, -1)
    for m in range(OWN // 2):
        at = FAR_W + m * LANES
        far_rows[:, at : at + LANES] = jnp.where(
            first_lanes,
            jnp.broadcast_to(lists[:, 2 * m : 2 * m + 1], (8, LANES)),
            jnp.broadcast_to(lists[:, 2 * m + 1 : 2 * m + 2], (8, LANES)),
        )
    lane_leaf = lax.broadcasted_iota(jnp.int32, (8, span), 1) // RANK

    def coupling(m):
        at = m * LANES
        to = at + LANES
        slot = m % BUFFERS

        def evaluate():
            values = lax.rsqrt(dot(sources[at : at + LANES, :], targets[:, to : to + span]))
            high[slot], low[slot] = split(values)

        def multiply():
            pair = coeffs[:, at : at + LANES]
            s_high, s_low = split(
                jnp.concatenate([jnp.where(first_lanes, pair, 0.0), jnp.where(first_lanes, 0.0, pair)], axis=0)
            )
            got = [dot(jnp.concatenate([s_high, s_low], axis=0), high[slot]), dot(s_high, low[slot])]
            if 2 * m >= FREACH:
                masked = []
                for i in range(2):
                    column = lists[:, 2 * m + i - FREACH : 2 * m + i - FREACH + 1]
                    hit = (lane_leaf + (2 * m + 2) == column).astype(jnp.float32)
                    masked.append(coeffs[:, to : to + span] * jnp.max(hit, axis=0, keepdims=True))
                t_high, t_low = split(jnp.concatenate(masked, axis=0))
                got.append(dot(jnp.concatenate([t_high, t_low], axis=0), high[slot], NT))
                got.append(dot(t_high, low[slot], NT))
            return got

        def add(got):
            forward = got[0][:16] + got[0][16:] + got[1]
            for i in range(2):
                hit = (far_rows[:, to : to + span] == 2 * m + i).astype(jnp.float32)
                hit = jnp.max(hit, axis=0, keepdims=True)
                down[:, to : to + span] += forward[8 * i : 8 * i + 8] * hit
            if len(got) > 2:
                reverse = got[2][:16] + got[2][16:] + got[3]
                down[:, at : at + LANES] += jnp.where(first_lanes, reverse[:8], reverse[8:])

        return evaluate, multiply, add

    steps = [coupling(m) for m in range((FREACH + OWN) // 2)]
    steps += edges(0, from_left) + edges(1, from_right)
    products = {}
    for i in range(len(steps) + AHEAD + 1):
        if i == (FREACH + OWN) // 2:
            for copy in copies:
                copy.wait()
        if i < len(steps):
            steps[i][0]()
        if 0 <= i - AHEAD < len(steps):
            products[i - AHEAD] = steps[i - AHEAD][1]()
        if 0 <= i - AHEAD - 1:
            steps[i - AHEAD - 1][2](products.pop(i - AHEAD - 1))

    plane = group // PLANE
    entries, kept = [], []
    for slot in range(FAR1):
        f = far_cluster[0, slot].astype(jnp.int32)
        valid = f >= 0
        f = jnp.where(valid, f, cluster)
        mine = f // (PLANE * NSUB) == plane
        place = lax.rem(f, PLANE * NSUB)
        e = jnp.where(mine, table[place], beyond[place])
        entries.append(e)
        kept.append(e * valid.astype(jnp.float32))
    parents, sources = [], []
    for m in range(len(entries) // 2):
        a, b = 2 * m, 2 * m + 1
        parents.append(jnp.where(first_lanes, kept[a], pltpu.roll(kept[b], RANK, 1)))
        sources.append(jnp.where(first_lanes, pltpu.roll(entries[a], RANK, 1), entries[b]))
    parents = jnp.concatenate(parents, axis=1)
    sources = jnp.concatenate(sources, axis=1)
    mine = table[lax.rem(cluster, PLANE * NSUB)].T[RANK : 2 * RANK]
    values = block_values(
        [mine[:, c : c + 1] for c in range(3)], [sources[c : c + 1, :] for c in range(3)]
    )
    coupled = dot3(parents, values, NT)

    pairs = range(OWN // 2)
    lowered = [dot3(coupled, jnp.reshape(transfer[2 * m : 2 * m + 2], (2 * RANK, RANK)), NT) for m in pairs]
    parts = []
    for m in pairs:
        pair = lowered[m] + down[:, FAR_W + m * LANES : FAR_W + (m + 1) * LANES]
        parts.append(
            split(jnp.concatenate([jnp.where(first_lanes, pair, 0.0), jnp.where(first_lanes, 0.0, pair)], axis=0))
        )
    far = [
        dot(jnp.concatenate(parts[m], axis=0), jnp.reshape(basis[2 * m : 2 * m + 2], (2 * RANK, LEAF)))
        for m in pairs
    ]
    for m in pairs:
        value = far[m][:16] + far[m][16:]
        for i in range(2):
            at = (2 * m + i) * LEAF
            out[:, at : at + LEAF] += value[8 * i : 8 * i + 8]


def shards(
    points, charges, order, basis, transfer, leaf_proxy, cluster_proxy, near, far_leaf, far_cluster
):
    vmem = pl.BlockSpec(memory_space=pltpu.VMEM)
    smem = pl.BlockSpec(memory_space=pltpu.SMEM)
    hbm = pl.BlockSpec(memory_space=pltpu.HBM)
    params = pltpu.CompilerParams(vmem_limit_bytes=48 * 2**20)
    f32 = jnp.float32
    leaf_proxy = leaf_proxy.transpose(1, 0, 2)
    cluster_proxy = cluster_proxy.transpose(1, 0, 2)
    near, far_leaf = near.transpose(1, 0), far_leaf.transpose(1, 0)
    given = (charges, points, order.reshape(PTS // LANES, LANES), basis, transfer, leaf_proxy, cluster_proxy, far_cluster)
    size = PLANE * NSUB
    own, inner, outer, spread = pl.pallas_call(
        prepare_kernel,
        in_specs=[hbm] * 8,
        out_specs=[vmem] * 4,
        out_shape=[
            jax.ShapeDtypeStruct((8, OWN_W), f32),
            jax.ShapeDtypeStruct((8, MSG), f32),
            jax.ShapeDtypeStruct((8, MSG), f32),
            jax.ShapeDtypeStruct((size, NRHS, LANES), f32),
        ],
        scratch_shapes=[pltpu.VMEM((2 * NRHS, PTS), jnp.bfloat16), pltpu.VMEM((NRHS, LANES), f32)]
        + [pltpu.VMEM(a.shape, a.dtype) for a in given]
        + [pltpu.SemaphoreType.DMA((8,))],
        name="prepare",
    )(*given)

    axes = ("leaf", "sub")
    groups, count = lax.axis_size("leaf"), lax.axis_size(axes)
    table = lax.all_to_all(
        spread, axes, 0, 0, tiled=True,
        axis_index_groups=[list(range(i, i + size)) for i in range(0, count, size)],
    )
    outer = lax.ppermute(outer, axes, [(i, ((i + 1) ^ 1) - 1) for i in range(1, count - 1)])
    inner = lax.ppermute(inner, axes, [(i, i ^ 1) for i in range(count)])
    shift = [(g - PLANE, g) for g in range(PLANE, groups) if g % PLANE < HALF]
    shift += [(g + PLANE, g) for g in range(groups - PLANE) if g % PLANE >= HALF]
    beyond = lax.ppermute(table, "leaf", shift)
    total = pl.pallas_call(
        near_kernel,
        in_specs=[hbm, vmem],
        out_specs=vmem,
        out_shape=jax.ShapeDtypeStruct((NRHS, PTS), f32),
        scratch_shapes=[
            pltpu.VMEM((8, PTS), jnp.bfloat16),
            pltpu.VMEM((PTS, 64), jnp.bfloat16),
            pltpu.VMEM((64, PTS), jnp.bfloat16),
            pltpu.VMEM((BUFFERS, REACH + 1, LEAF, LEAF), jnp.bfloat16),
            pltpu.SMEM(near.shape, near.dtype),
            pltpu.SemaphoreType.DMA,
        ],
        cost_estimate=pl.CostEstimate(flops=9 * 10**9, bytes_accessed=10**6, transcendentals=3 * 10**6),
        compiler_params=params,
        name="near_field",
    )(near, own)
    far_window = OWN + 2 * FREACH
    return pl.pallas_call(
        product_kernel,
        in_specs=[hbm] + [vmem] * 9,
        out_specs=vmem,
        out_shape=jax.ShapeDtypeStruct((NRHS, PTS), f32),
        scratch_shapes=[
            pltpu.VMEM((NRHS, far_window * RANK), f32),
            pltpu.VMEM((8, far_window * RANK), f32),
            pltpu.VMEM((far_window * RANK, 64), jnp.bfloat16),
            pltpu.VMEM((64, far_window * RANK), jnp.bfloat16),
            pltpu.VMEM((2 * REACH, LEAF, REACH * LEAF), jnp.bfloat16),
            pltpu.VMEM((BUFFERS, 2 * RANK, 3 * LANES), jnp.bfloat16),
            pltpu.VMEM((BUFFERS, 2 * RANK, 3 * LANES), jnp.bfloat16),
            pltpu.VMEM((8, far_window * RANK), jnp.int32),
            pltpu.SMEM(near.shape, near.dtype),
            pltpu.SMEM((8, LANES), f32),
            pltpu.SemaphoreType.DMA((2,)),
        ],
        compiler_params=params,
        name="product",
    )(near, far_leaf, transfer, basis, own, outer, inner, total, table, beyond)


def solution(mesh):
    in_specs = (
        P(None, ("leaf", "sub")),
        P(None, ("leaf", "sub")),
        P(("leaf", "sub")),
        P(("leaf", "sub"), None, None),
        P(("leaf", "sub"), None, None),
        P(("leaf", "sub"), None, None),
        P(("leaf", "sub"), None, None),
        P(("leaf", "sub"), None),
        P(("leaf", "sub"), None),
        P(("leaf", "sub"), None),
    )
    out_specs = P(None, ("leaf", "sub"))
    return jax.shard_map(shards, mesh=mesh, in_specs=in_specs, out_specs=out_specs, check_vma=False)
```

```python
import jax
import jax.numpy as jnp
from jax import lax
from jax.experimental import pallas as pl
from jax.experimental.pallas import tpu as pltpu
from jax.sharding import PartitionSpec as P

LEAF = 256
RANK = 64
NRHS = 8
OWN = 16
REACH = 2
FREACH = 6
PLANE = 8
HALF = PLANE // 2
NSUB = 4
FAR1 = 16
PTS = OWN * LEAF
RANKS = OWN * RANK
LANES = 128
BUFFERS = 6
LATER = 3
AHEAD = 3
SCALE = 16.0
SHIFT = 2.56

NEAR_W = REACH * LEAF
FAR_W = FREACH * RANK
MSG = 2 * NEAR_W + 2 * FAR_W
AT_CHARGES, AT_POINTS, AT_COEFFS, AT_PROXY = 0, PTS, 2 * PTS, 2 * PTS + RANKS
AT_LIST = 2 * PTS + 2 * RANKS
OWN_W = AT_LIST + LANES

NT = (((1,), (1,)), ((), ()))
NN = (((1,), (0,)), ((), ()))


def dot(a, b, dims=NN):
    return lax.dot_general(a, b, dims, preferred_element_type=jnp.float32)


def split(x):
    high = x.astype(jnp.bfloat16)
    return high, (x - high.astype(jnp.float32)).astype(jnp.bfloat16)


def dot3(a, b, dims=NN):
    rows = a.shape[0]
    a_high, a_low = split(a)
    b_high, b_low = split(b)
    both = dot(jnp.concatenate([a_high, a_low], axis=0), b_high, dims)
    return both[:rows] + both[rows:] + dot(a_high, b_low, dims)


ALONG_LANES = lax.GatherDimensionNumbers(
    offset_dims=(), collapsed_slice_dims=(1,), start_index_map=(1,), operand_batching_dims=(0,),
    start_indices_batching_dims=(0,),
)


def picked(source, index, count, dtype):
    low = jnp.bitwise_and(index, dtype(LANES - 1))[..., None]
    bits, k = [], 1
    while k < count:
        bits.append(jnp.bitwise_and(index, dtype(k * LANES)) != 0)
        k *= 2

    def among(first, level):
        if level == 0:
            return lax.gather(
                source(first), low, ALONG_LANES, (1, 1), mode=lax.GatherScatterMode.PROMISE_IN_BOUNDS
            )
        size = 1 << (level - 1)
        return jnp.where(bits[level - 1], among(first + size, level - 1), among(first, level - 1))

    return among(0, len(bits))


def prepare_kernel(
    charges, points, order, basis, transfer, leaf_proxy, cluster_proxy, far_cluster,
    own, inner, outer, spread,
    twice, entry, charges_in, points_in, order_in, basis_in, transfer_in, leaf_proxy_in, cluster_proxy_in, far_cluster_in, sems,
):
    copies = [
        pltpu.make_async_copy(a, b, sems.at[i])
        for i, (a, b) in enumerate(
            (
                (order, order_in), (charges, charges_in), (points, points_in), (leaf_proxy, leaf_proxy_in),
                (cluster_proxy, cluster_proxy_in), (far_cluster, far_cluster_in), (basis, basis_in),
                (transfer, transfer_in),
            )
        )
    ]
    for copy in copies:
        copy.start()
    own[:, AT_PROXY : AT_PROXY + RANKS] = jnp.zeros((8, RANKS), jnp.float32)
    entry[...] = jnp.zeros((NRHS, LANES), jnp.float32)
    own[:, AT_POINTS : AT_POINTS + PTS] = jnp.zeros((8, PTS), jnp.float32)
    for copy in copies[:3]:
        copy.wait()
    blocks = PTS // LANES
    both = charges_in[...].astype(jnp.float32)
    twice[...] = jnp.concatenate([both, both], axis=0).astype(jnp.bfloat16)

    for i in range(blocks // 2):
        index = jnp.concatenate(
            [jnp.broadcast_to(order_in[2 * i + k : 2 * i + k + 1, :], (NRHS, LANES)) for k in range(2)], axis=0
        ).astype(jnp.int16)
        got = picked(
            lambda k: twice[:, k * LANES : (k + 1) * LANES], index, blocks, jnp.int16
        ).astype(jnp.float32)
        for k in range(2):
            own[:, (2 * i + k) * LANES : (2 * i + k + 1) * LANES] = got[NRHS * k : NRHS * (k + 1)]

    for copy in copies[3:]:
        copy.wait()
    for g in range(OWN):
        at = AT_PROXY + g * RANK
        own[0:3, at : at + RANK] = leaf_proxy_in[:, g, :] * SCALE
    own[:, AT_LIST:] = jnp.zeros((8, LANES), jnp.float32)
    own[0:1, AT_LIST : AT_LIST + far_cluster_in.shape[1]] = far_cluster_in[...].astype(jnp.float32)

    first_half = lax.broadcasted_iota(jnp.int32, (NRHS, LANES), 1) < RANK
    parent = jnp.zeros((NRHS, RANK), jnp.float32)
    for j in range(blocks // 8):
        pairs = range(2 * j, 2 * j + 2)
        both = [
            dot(
                jnp.concatenate(
                    [own[:, g * LEAF : (g + 1) * LEAF].astype(jnp.bfloat16) for g in (2 * m, 2 * m + 1)], axis=0
                ),
                jnp.reshape(basis_in[2 * m : 2 * m + 2], (2 * RANK, LEAF)),
                NT,
            )
            for m in pairs
        ]
        index = order_in[8 * j : 8 * j + 8, :]
        for c in range(3):
            got = picked(
                lambda k: jnp.broadcast_to(points_in[c : c + 1, k * LANES : (k + 1) * LANES], (8, LANES)),
                index, blocks, jnp.int32,
            ) * SCALE
            for s in range(8):
                at = AT_POINTS + (8 * j + s) * LANES
                own[c : c + 1, at : at + LANES] = got[s : s + 1]
        for m, pair in zip(pairs, both):
            coeffs = jnp.where(first_half, pair[:NRHS], pair[NRHS:])
            own[:, AT_COEFFS + m * LANES : AT_COEFFS + (m + 1) * LANES] = coeffs
            parent += dot3(coeffs, jnp.reshape(transfer_in[2 * m : 2 * m + 2], (2 * RANK, RANK)))

    entry[:, 0:RANK] = parent
    entry[0:3, RANK : 2 * RANK] = cluster_proxy_in[:, 0, :] * SCALE

    for place in range(PLANE * NSUB):
        spread[place] = entry[...]

    odd = lax.rem(lax.axis_index("sub"), 2) == 1
    at = 0
    for start, whole, width in (
        (AT_CHARGES, PTS, NEAR_W), (AT_POINTS, PTS, NEAR_W),
        (AT_COEFFS, RANKS, FAR_W), (AT_PROXY, RANKS, FAR_W),
    ):
        low = own[:, start : start + width]
        high = own[:, start + whole - width : start + whole]
        inner[:, at : at + width] = jnp.where(odd, low, high)
        outer[:, at : at + width] = jnp.where(odd, high, low)
        at += width


def block_values(columns, rows):
    d0 = columns[0] - rows[0]
    d1 = columns[1] - rows[1]
    d2 = columns[2] - rows[2]
    return lax.rsqrt(d0 * d0 + d1 * d1 + d2 * d2 + SHIFT)


def features(points, as_source):
    row = lax.broadcasted_iota(jnp.int32, points.shape, 0)
    h = jnp.floor(points * 2.0 + 0.5) * 0.5
    l = points - h
    l1 = l.astype(jnp.bfloat16).astype(jnp.float32)
    l2 = l - l1
    n = jnp.sum(h * h, axis=0, keepdims=True)
    n1 = jnp.floor(n * (1 / 128) + 0.5) * 128.0
    n2 = n - n1
    s = jnp.sum((2.0 * h + l) * l, axis=0, keepdims=True) + SHIFT / 2
    s1 = s.astype(jnp.bfloat16).astype(jnp.float32)
    s2 = (s - s1).astype(jnp.bfloat16).astype(jnp.float32)
    s3 = s - s1 - s2

    def stack(vector, *others):
        for i, other in enumerate(others):
            vector = jnp.where(row == 3 + i, other, vector)
        return vector

    if as_source:
        groups = [
            stack(h, n1, n2, 1.0, 1.0), stack(h, s1, s2, s3, 1.0, 1.0), stack(h, 1.0), l1, l2, l1, l1, l2
        ]
    else:
        h, l1, l2 = -2.0 * h, -2.0 * l1, -2.0 * l2
        groups = [
            stack(h, 1.0, 1.0, n1, n2), stack(l1, 1.0, 1.0, 1.0, s1, s2), stack(l2, s3), h, h, l1, l2, l1
        ]
    return jnp.concatenate(groups, axis=0).astype(jnp.bfloat16)


def strip(sources, targets, block):
    for at in range(0, targets.shape[1], LEAF):
        block[:, at : at + LEAF] = lax.rsqrt(dot(sources, targets[:, at : at + LEAF])).astype(jnp.bfloat16)


def listing(near, first):
    def listed(target, h):
        hit = near[0, target] == first + h
        for slot in range(1, near.shape[0]):
            hit = jnp.logical_or(hit, near[slot, target] == first + h)
        return hit.astype(jnp.float32)

    return listed


def near_kernel(near_list, own, total, charges, sources, targets, block, near, sem):
    copy = pltpu.make_async_copy(near_list, near, sem)
    copy.start()
    first = (lax.axis_index("leaf") * NSUB + lax.axis_index("sub")) * OWN
    listed = listing(near, first)
    charges[...] = own[:, 0:PTS].astype(jnp.bfloat16)
    for t in range(PTS // LANES):
        points = own[:, PTS + t * LANES : PTS + (t + 1) * LANES]
        sources[t * LANES : (t + 1) * LANES, :] = features(points, True).T
        targets[:, t * LANES : (t + 1) * LANES] = features(points, False)
    copy.wait()

    sums = [0.0] * OWN
    for step in range(OWN + LATER):
        for d in range(REACH + 1):
            h = step
            if h + d < OWN:
                strip(
                    sources[h * LEAF : (h + 1) * LEAF, :],
                    targets[:, (h + d) * LEAF : (h + d + 1) * LEAF],
                    block.at[h % BUFFERS, d],
                )
            h = step - LATER
            if h >= 0 and h + d < OWN:
                here = slice(h * LEAF, (h + 1) * LEAF)
                there = slice((h + d) * LEAF, (h + d + 1) * LEAF)
                values = block[h % BUFFERS, d]
                sums[h + d] += dot(charges[:, here], values) * listed(h + d, h)
                if d > 0:
                    sums[h] += dot(charges[:, there], values, NT) * listed(h, h + d)
        if step >= LATER:
            total[:, (step - LATER) * LEAF : (step - LATER + 1) * LEAF] = sums[step - LATER]


def product_kernel(
    near_list, far_leaf, transfer, basis, own, outer, inner, total, table, beyond,
    out,
    down, coeffs, sources, targets, block, high, low, far_rows, near, far_cluster, sems,
):
    copies = [
        pltpu.make_async_copy(a, b, sems.at[i])
        for i, (a, b) in enumerate(((near_list, near), (own.at[:, AT_LIST:], far_cluster)))
    ]
    for copy in copies:
        copy.start()
    group = lax.axis_index("leaf")
    cluster = group * NSUB + lax.axis_index("sub")
    first = cluster * OWN
    odd = lax.rem(lax.axis_index("sub"), 2) == 1
    from_left = jnp.where(odd, inner[...], outer[...])
    from_right = jnp.where(odd, outer[...], inner[...])

    out[...] = total[...]
    down[...] = jnp.zeros_like(down)
    at = 2 * NEAR_W
    pieces = []
    for start, width in ((AT_COEFFS, FAR_W), (AT_PROXY, FAR_W)):
        pieces.append((from_left[:, at : at + width], own[:, start : start + RANKS], from_right[:, at : at + width]))
        at += width
    coeffs[...] = jnp.concatenate(pieces[0], axis=1)
    for t, proxies in enumerate(pieces[1]):
        at = (0, FAR_W, FAR_W + RANKS)[t]
        sources[at : at + proxies.shape[1], :] = features(proxies, True).T
        targets[:, at : at + proxies.shape[1]] = features(proxies, False)
    listed = listing(near, first)

    def edges(side, message):
        at = 0 if side == 0 else PTS - NEAR_W
        columns = features(message[:, NEAR_W : 2 * NEAR_W], True).T
        rows = features(own[:, PTS + at : PTS + at + NEAR_W], False)
        steps = []
        for i in range(REACH):
            h = i - REACH if side == 0 else OWN + i
            leaves = [g for g in range(OWN) if abs(g - h) <= REACH]
            skip, width = leaves[0] * LEAF - at, len(leaves) * LEAF
            values = block.at[REACH * side + i]

            def evaluate(i=i, values=values, skip=skip, width=width):
                strip(columns[i * LEAF : (i + 1) * LEAF], rows[:, skip : skip + width], values)

            def multiply(i=i, values=values, width=width):
                return dot(message[:, i * LEAF : (i + 1) * LEAF].astype(jnp.bfloat16), values[:, 0:width])

            def add(forward, h=h, leaves=leaves):
                for k, g in enumerate(leaves):
                    out[:, g * LEAF : (g + 1) * LEAF] += forward[:, k * LEAF : (k + 1) * LEAF] * listed(g, h)

            steps.append((evaluate, multiply, add))
        return steps

    span = 3 * LANES
    first_lanes = lax.broadcasted_iota(jnp.int32, (NRHS, LANES), 1) < RANK
    lists = jnp.where(far_leaf[...] >= 0, far_leaf[...] - first + FREACH, -1)
    far_rows[...] = jnp.full_like(far_rows, -1)
    for m in range(OWN // 2):
        at = FAR_W + m * LANES
        far_rows[:, at : at + LANES] = jnp.where(
            first_lanes,
            jnp.broadcast_to(lists[:, 2 * m : 2 * m + 1], (8, LANES)),
            jnp.broadcast_to(lists[:, 2 * m + 1 : 2 * m + 2], (8, LANES)),
        )
    lane_leaf = lax.broadcasted_iota(jnp.int32, (8, span), 1) // RANK

    def coupling(m):
        at = m * LANES
        to = at + LANES
        slot = m % BUFFERS

        def evaluate():
            values = lax.rsqrt(dot(sources[at : at + LANES, :], targets[:, to : to + span]))
            high[slot], low[slot] = split(values)

        def multiply():
            pair = coeffs[:, at : at + LANES]
            s_high, s_low = split(
                jnp.concatenate([jnp.where(first_lanes, pair, 0.0), jnp.where(first_lanes, 0.0, pair)], axis=0)
            )
            got = [dot(jnp.concatenate([s_high, s_low], axis=0), high[slot]), dot(s_high, low[slot])]
            if 2 * m >= FREACH:
                masked = []
                for i in range(2):
                    column = lists[:, 2 * m + i - FREACH : 2 * m + i - FREACH + 1]
                    hit = (lane_leaf + (2 * m + 2) == column).astype(jnp.float32)
                    masked.append(coeffs[:, to : to + span] * jnp.max(hit, axis=0, keepdims=True))
                t_high, t_low = split(jnp.concatenate(masked, axis=0))
                got.append(dot(jnp.concatenate([t_high, t_low], axis=0), high[slot], NT))
                got.append(dot(t_high, low[slot], NT))
            return got

        def add(got):
            forward = got[0][:16] + got[0][16:] + got[1]
            for i in range(2):
                hit = (far_rows[:, to : to + span] == 2 * m + i).astype(jnp.float32)
                hit = jnp.max(hit, axis=0, keepdims=True)
                down[:, to : to + span] += forward[8 * i : 8 * i + 8] * hit
            if len(got) > 2:
                reverse = got[2][:16] + got[2][16:] + got[3]
                down[:, at : at + LANES] += jnp.where(first_lanes, reverse[:8], reverse[8:])

        return evaluate, multiply, add

    steps = [coupling(m) for m in range((FREACH + OWN) // 2)]
    steps += edges(0, from_left) + edges(1, from_right)
    def couple():
        plane = group // PLANE
        entries, kept = [], []
        for slot in range(FAR1):
            f = far_cluster[0, slot].astype(jnp.int32)
            valid = f >= 0
            f = jnp.where(valid, f, cluster)
            mine = f // (PLANE * NSUB) == plane
            place = lax.rem(f, PLANE * NSUB)
            e = jnp.where(mine, table[place], beyond[place])
            entries.append(e)
            kept.append(e * valid.astype(jnp.float32))
        parents, sources = [], []
        for m in range(len(entries) // 2):
            a, b = 2 * m, 2 * m + 1
            parents.append(jnp.where(first_lanes, kept[a], pltpu.roll(kept[b], RANK, 1)))
            sources.append(jnp.where(first_lanes, pltpu.roll(entries[a], RANK, 1), entries[b]))
        parents = jnp.concatenate(parents, axis=1)
        sources = jnp.concatenate(sources, axis=1)
        mine = table[lax.rem(cluster, PLANE * NSUB)].T[RANK : 2 * RANK]
        values = block_values(
            [mine[:, c : c + 1] for c in range(3)], [sources[c : c + 1, :] for c in range(3)]
        )
        return dot3(parents, values, NT)

    products = {}
    for i in range(len(steps) + AHEAD + 1):
        if i == (FREACH + OWN) // 2:
            for copy in copies:
                copy.wait()
        if i == (FREACH + OWN) // 2 + 1:
            coupled = couple()
        if i < len(steps):
            steps[i][0]()
        if 0 <= i - AHEAD < len(steps):
            products[i - AHEAD] = steps[i - AHEAD][1]()
        if 0 <= i - AHEAD - 1:
            steps[i - AHEAD - 1][2](products.pop(i - AHEAD - 1))

    pairs = range(OWN // 2)
    lowered = [dot3(coupled, jnp.reshape(transfer[2 * m : 2 * m + 2], (2 * RANK, RANK)), NT) for m in pairs]
    parts = []
    for m in pairs:
        pair = lowered[m] + down[:, FAR_W + m * LANES : FAR_W + (m + 1) * LANES]
        parts.append(
            split(jnp.concatenate([jnp.where(first_lanes, pair, 0.0), jnp.where(first_lanes, 0.0, pair)], axis=0))
        )
    far = [
        dot(jnp.concatenate(parts[m], axis=0), jnp.reshape(basis[2 * m : 2 * m + 2], (2 * RANK, LEAF)))
        for m in pairs
    ]
    for m in pairs:
        value = far[m][:16] + far[m][16:]
        for i in range(2):
            at = (2 * m + i) * LEAF
            out[:, at : at + LEAF] += value[8 * i : 8 * i + 8]


def shards(
    points, charges, order, basis, transfer, leaf_proxy, cluster_proxy, near, far_leaf, far_cluster
):
    vmem = pl.BlockSpec(memory_space=pltpu.VMEM)
    smem = pl.BlockSpec(memory_space=pltpu.SMEM)
    hbm = pl.BlockSpec(memory_space=pltpu.HBM)
    params = pltpu.CompilerParams(vmem_limit_bytes=48 * 2**20)
    f32 = jnp.float32
    leaf_proxy = leaf_proxy.transpose(1, 0, 2)
    cluster_proxy = cluster_proxy.transpose(1, 0, 2)
    near, far_leaf = near.transpose(1, 0), far_leaf.transpose(1, 0)
    given = (charges, points, order.reshape(PTS // LANES, LANES), basis, transfer, leaf_proxy, cluster_proxy, far_cluster)
    size = PLANE * NSUB
    own, inner, outer, spread = pl.pallas_call(
        prepare_kernel,
        in_specs=[hbm] * 8,
        out_specs=[vmem] * 4,
        out_shape=[
            jax.ShapeDtypeStruct((8, OWN_W), f32),
            jax.ShapeDtypeStruct((8, MSG), f32),
            jax.ShapeDtypeStruct((8, MSG), f32),
            jax.ShapeDtypeStruct((size, NRHS, LANES), f32),
        ],
        scratch_shapes=[pltpu.VMEM((2 * NRHS, PTS), jnp.bfloat16), pltpu.VMEM((NRHS, LANES), f32)]
        + [pltpu.VMEM(a.shape, a.dtype) for a in given]
        + [pltpu.SemaphoreType.DMA((8,))],
        name="prepare",
    )(*given)

    axes = ("leaf", "sub")
    groups, count = lax.axis_size("leaf"), lax.axis_size(axes)
    table = lax.all_to_all(
        spread, axes, 0, 0, tiled=True,
        axis_index_groups=[list(range(i, i + size)) for i in range(0, count, size)],
    )
    outer = lax.ppermute(outer, axes, [(i, ((i + 1) ^ 1) - 1) for i in range(1, count - 1)])
    inner = lax.ppermute(inner, axes, [(i, i ^ 1) for i in range(count)])
    shift = [(g - PLANE, g) for g in range(PLANE, groups) if g % PLANE < HALF]
    shift += [(g + PLANE, g) for g in range(groups - PLANE) if g % PLANE >= HALF]
    beyond = lax.ppermute(table, "leaf", shift)
    total = pl.pallas_call(
        near_kernel,
        in_specs=[hbm, vmem],
        out_specs=vmem,
        out_shape=jax.ShapeDtypeStruct((NRHS, PTS), f32),
        scratch_shapes=[
            pltpu.VMEM((8, PTS), jnp.bfloat16),
            pltpu.VMEM((PTS, 64), jnp.bfloat16),
            pltpu.VMEM((64, PTS), jnp.bfloat16),
            pltpu.VMEM((BUFFERS, REACH + 1, LEAF, LEAF), jnp.bfloat16),
            pltpu.SMEM(near.shape, near.dtype),
            pltpu.SemaphoreType.DMA,
        ],
        cost_estimate=pl.CostEstimate(flops=9 * 10**9, bytes_accessed=10**6, transcendentals=3 * 10**6),
        compiler_params=params,
        name="near_field",
    )(near, own)
    far_window = OWN + 2 * FREACH
    return pl.pallas_call(
        product_kernel,
        in_specs=[hbm] + [vmem] * 9,
        out_specs=vmem,
        out_shape=jax.ShapeDtypeStruct((NRHS, PTS), f32),
        scratch_shapes=[
            pltpu.VMEM((NRHS, far_window * RANK), f32),
            pltpu.VMEM((8, far_window * RANK), f32),
            pltpu.VMEM((far_window * RANK, 64), jnp.bfloat16),
            pltpu.VMEM((64, far_window * RANK), jnp.bfloat16),
            pltpu.VMEM((2 * REACH, LEAF, REACH * LEAF), jnp.bfloat16),
            pltpu.VMEM((BUFFERS, 2 * RANK, 3 * LANES), jnp.bfloat16),
            pltpu.VMEM((BUFFERS, 2 * RANK, 3 * LANES), jnp.bfloat16),
            pltpu.VMEM((8, far_window * RANK), jnp.int32),
            pltpu.SMEM(near.shape, near.dtype),
            pltpu.SMEM((8, LANES), f32),
            pltpu.SemaphoreType.DMA((2,)),
        ],
        compiler_params=params,
        name="product",
    )(near, far_leaf, transfer, basis, own, outer, inner, total, table, beyond)


def solution(mesh):
    in_specs = (
        P(None, ("leaf", "sub")),
        P(None, ("leaf", "sub")),
        P(("leaf", "sub")),
        P(("leaf", "sub"), None, None),
        P(("leaf", "sub"), None, None),
        P(("leaf", "sub"), None, None),
        P(("leaf", "sub"), None, None),
        P(("leaf", "sub"), None),
        P(("leaf", "sub"), None),
        P(("leaf", "sub"), None),
    )
    out_specs = P(None, ("leaf", "sub"))
    return jax.shard_map(shards, mesh=mesh, in_specs=in_specs, out_specs=out_specs, check_vma=False)
```
